256 devices in a mesh: rep: 4 (over x_lo, core), fsdp: 64 (over y, x_hi, z).
Axes of the slice: x: 4 (x_hi: 2, x_lo: 2; x = x_hi * 2 + x_lo), y: 4, z: 8, core: 2. Of those that a mesh axis runs over, the one named last changes fastest.
Arguments:
- tokens: bfloat16 [196608, 4096], P(('rep', 'fsdp')), may hold values from -24 to 24
- cotangent: bfloat16 [196608, 512], P(('rep', 'fsdp')), may hold values from -0.013671875 to 0.013671875
- policy: float32 [4096, 512], P('fsdp'), may hold values from -0.09375 to 0.09375
- anchor: float32 [4096, 512], P('fsdp'), may hold values from -0.09375 to 0.09375
- moment: float32 [4096, 512], P('fsdp'), may hold values from -3 to 3
- second: float32 [4096, 512], P('fsdp'), may hold values from 0.25 to 4
- readout: float32 [512], replicated, may hold values from -6 to 6
- pair_index: int32 [512, 2], P(('rep', 'fsdp')), may hold values from 0 to 1023, as said below
- noisy_flags: int32 [512], P(('rep', 'fsdp')), may hold values 0 or 1
Outputs:
- policy_next: float32 [4096, 512], P('fsdp')
- anchor_next: float32 [4096, 512], P('fsdp')
- moment_next: float32 [4096, 512], P('fsdp')
- second_next: float32 [4096, 512], P('fsdp')
- pair_loss: float32 [512], P(('rep', 'fsdp'))
The draws below stay inside these ranges and needn't reach their ends.
Inputs may be any that keep to these rules, and one draw needn't show every extreme that they name: Each of the 1024 sequences appears exactly once in pair_index.
All inputs are finite; a program needn't handle non-finite values. No bound on the sum of `noisy_flags` on one device may be relied on, other than what follows from the above.
Results may differ from the reference program's by a relative error of at most 0.0025.
Values may be sent and summed in bfloat16 or wider, within the bound.
No kernel may reach another device: no remote copies, remote signals or barrier semaphores. Data moves between devices by JAX's collectives and lax.ppermute only.
A program may use at most 64 MiB of HBM per device.

```python
import math
import jax
import jax.numpy as jnp
from jax import lax

D = 4096
DV = 512
LEN = 192
TOKENS = 196608
NSEQ = 1024
PAIRS = 512


def draw_pair_index(key, part):
    shuffled = jax.random.permutation(jax.random.fold_in(key, 11), NSEQ)
    return shuffled.astype(jnp.int32).reshape(PAIRS, 2)


def touch_ends(values, own_key, least, high):
    longest = values.shape.index(max(values.shape))
    spots = []
    for shift in (0, 1):
        where = [jax.random.randint(jax.random.fold_in(own_key, axis), (), 0, length) for axis, length in enumerate(values.shape)]
        where[longest] = (where[longest] + shift) % values.shape[longest]
        spots.append(tuple(where))
    return values.at[spots[0]].set(least).at[spots[1]].set(high)


def strengthened(entries, rng, source, target, parts, factor):
    owner, partner = [(jnp.arange(entries.shape[position]) // (entries.shape[position] // parts)).reshape([-1 if axis == position else 1 for axis in range(entries.ndim)]) for position in (source, target)]
    chosen = jax.random.permutation(rng, parts)[partner]
    strong = (owner == chosen) | (owner == (partner + parts // 2) % parts)
    return jnp.where(strong, factor * entries, entries)


def block_levels(key, dims, cuts, low, top_value):
    def one(axis_at, shards_of):
        heights = jax.random.uniform(jax.random.fold_in(jax.random.fold_in(key, 6), axis_at), (shards_of,), jnp.float32, low / len(cuts), top_value / len(cuts))
        return jnp.repeat(jnp.exp(heights), dims[axis_at] // shards_of).reshape((-1,) + (1,) * (len(dims) - axis_at - 1))

    loudness = one(*cuts[0])
    for cut in cuts[1:]:
        loudness = loudness * one(*cut)
    return loudness


def noise(key, dims, deviation, limit, shards=(), held_as=jnp.bfloat16):
    factor_of = block_levels(key, dims, shards, -0.22, 0.18) if shards else 1.0
    array = jax.random.normal(key, dims, jnp.float32) * deviation * factor_of
    return jnp.minimum(jnp.maximum(array, -limit), limit).astype(held_as)


def bell_draw_with(stream_key, dims, scale, limit, cuts, heavy, kind=jnp.bfloat16):
    values = scale * jax.random.normal(stream_key, dims, jnp.float32)
    if cuts:
        values = values * block_levels(stream_key, dims, cuts, -0.22, 0.18)
    return jnp.clip(strengthened(values, jax.random.fold_in(stream_key, 3), *heavy), -limit, limit).astype(kind)


def setup_inputs(seed: int = 0) -> dict:
    key_of = jax.random.split(jax.random.key(seed), 10)
    return {
        "tokens": bell_draw_with(key_of[0], (TOKENS, D), 1.0, 24.0, ((0, 256),), (0, 1, 256, 6.0)),
        "cotangent": noise(key_of[1], (TOKENS, DV), TOKENS ** -0.5, 0.013671875, ((0, 256),)),
        "policy": noise(key_of[2], (D, DV), D ** -0.5, 0.09375, ((0, 64),), jnp.float32),
        "anchor": noise(key_of[3], (D, DV), D ** -0.5, 0.09375, ((0, 64),), jnp.float32),
        "moment": noise(key_of[4], (D, DV), 0.5, 3.0, ((0, 64),), jnp.float32),
        "second": jnp.clip(jnp.exp(math.log(4.0) - 2.7725887 * jax.random.uniform(key_of[5], (D, DV), jnp.float32) ** block_levels(key_of[5], (D, DV), ((0, 64),), -0.2, 0.2)), 0.25, 4.0),
        "readout": noise(key_of[6], (DV,), 1.0, 6.0, (), jnp.float32),
        "pair_index": draw_pair_index(jax.random.fold_in(key_of[9], 71), 0),
        "noisy_flags": touch_ends((jax.random.randint(key_of[8], (PAIRS,), 0, 8) < 1).astype(jnp.int32), jax.random.fold_in(key_of[8], 1), 0, 1),
    }


beta_one = 0.9
beta_two = 0.95
step_count = 20
learn_rate = 0.003
adam_epsilon = 1e-08
blend_rate = 0.6
smoothing = 0.1

def adam_update(gradient, policy, anchor, moment, second):
    moment_new = beta_one * moment + (1.0 - beta_one) * gradient
    second_new = beta_two * second + (1.0 - beta_two) * gradient * gradient
    correct_one = 1.0 - beta_one ** step_count
    correct_two = 1.0 - beta_two ** step_count
    policy_new = policy - learn_rate * (moment_new / correct_one) / (jnp.sqrt(second_new / correct_two) + adam_epsilon)
    anchor_new = blend_rate * policy_new + (1.0 - blend_rate) * anchor
    return (policy_new, anchor_new, moment_new, second_new)

def token_scores(values, readout):
    return lax.optimization_barrier(jnp.sum(jax.nn.log_sigmoid(values * readout[None, :]), axis=1))

def sequence_margin(policy_values, anchor_values, readout, sequence_length):
    token_gap = token_scores(policy_values, readout) - token_scores(anchor_values, readout)
    return lax.optimization_barrier(jnp.mean(token_gap.reshape(-1, sequence_length), axis=1))

def pair_losses(margins, pair_index, noisy_flags):
    sequence_index = jnp.arange(margins.shape[0], dtype=jnp.int32)
    chosen = lax.optimization_barrier(jnp.sum(jnp.where(pair_index[:, 0:1] == sequence_index[None, :], margins[None, :], 0.0), axis=1))
    rejected = lax.optimization_barrier(jnp.sum(jnp.where(pair_index[:, 1:2] == sequence_index[None, :], margins[None, :], 0.0), axis=1))
    margin_gap = chosen - rejected
    logit_value = jnp.where(noisy_flags == 1, -margin_gap, margin_gap)
    return -(1.0 - smoothing) * jax.nn.log_sigmoid(logit_value) - smoothing * jax.nn.log_sigmoid(-logit_value)

def reference(tokens, cotangent, policy, anchor, moment, second, readout, pair_index, noisy_flags):
    gradient = lax.dot_general(tokens, cotangent, (((0,), (0,)), ((), ())), preferred_element_type=jnp.float32)
    policy_next, anchor_next, moment_next, second_next = adam_update(gradient, policy, anchor, moment, second)
    policy_values = jnp.dot(tokens, policy_next.astype(jnp.bfloat16), preferred_element_type=jnp.float32)
    anchor_values = jnp.dot(tokens, anchor_next.astype(jnp.bfloat16), preferred_element_type=jnp.float32)
    margins = sequence_margin(policy_values, anchor_values, readout, LEN)
    pair_loss = pair_losses(margins, pair_index, noisy_flags)
    return (policy_next, anchor_next, moment_next, second_next, pair_loss)
```

```python
import jax
import jax.numpy as jnp
from jax import lax
from jax.sharding import Mesh
from jax.sharding import PartitionSpec as P

LEN = 192


beta_one = 0.9
beta_two = 0.95
step_count = 20
learn_rate = 0.003
adam_epsilon = 1e-08
blend_rate = 0.6
smoothing = 0.1

AXES = ("xlo", "core", "y", "xhi", "z")
PLANE = ("xlo", "y", "xhi")
SWAP = ((0, 1), (1, 0))


def adam_update(gradient, policy, anchor, moment, second):
    moment_new = beta_one * moment + (1.0 - beta_one) * gradient
    second_new = beta_two * second + (1.0 - beta_two) * gradient * gradient
    correct_one = 1.0 - beta_one**step_count
    correct_two = 1.0 - beta_two**step_count
    policy_new = policy - learn_rate * (moment_new / correct_one) / (
        jnp.sqrt(second_new / correct_two) + adam_epsilon
    )
    anchor_new = blend_rate * policy_new + (1.0 - blend_rate) * anchor
    return (policy_new, anchor_new, moment_new, second_new)


def token_scores(values, readout):
    return jnp.sum(jax.nn.log_sigmoid(values * readout[None, :]), axis=1)


def pair_losses(margins, pair_index, noisy_flags):
    sequence_index = jnp.arange(margins.shape[0], dtype=jnp.int32)
    chosen = jnp.sum(
        jnp.where(pair_index[:, 0:1] == sequence_index[None, :], margins[None, :], 0.0), axis=1
    )
    rejected = jnp.sum(
        jnp.where(pair_index[:, 1:2] == sequence_index[None, :], margins[None, :], 0.0), axis=1
    )
    margin_gap = chosen - rejected
    logit_value = jnp.where(noisy_flags == 1, -margin_gap, margin_gap)
    return -(1.0 - smoothing) * jax.nn.log_sigmoid(logit_value) - smoothing * jax.nn.log_sigmoid(
        -logit_value
    )


def gradient_product(tokens, cotangent):
    return lax.dot_general(
        tokens, cotangent, (((0,), (0,)), ((), ())), preferred_element_type=jnp.float32
    )


def shards(tokens, cotangent, policy, anchor, moment, second, readout, pair_index, noisy_flags):
    core = lax.axis_index("core")
    low = lax.axis_index("xlo")
    half = cotangent.shape[1] // 2
    rows = policy.shape[0] // 2
    features = tokens.shape[1]

    def columns(array, which):
        return lax.dynamic_slice_in_dim(array, which * half, half, axis=array.ndim - 1)

    def piece(array):
        return lax.dynamic_slice(array, (low * rows, core * half), (rows, half))

    anchor_cols = lax.all_gather(
        columns(anchor, core).astype(jnp.bfloat16), ("y", "xhi", "z"), axis=0, tiled=True
    )
    sent = gradient_product(tokens, columns(cotangent, 1 - core)).astype(jnp.bfloat16)
    arrived = lax.ppermute(sent, "core", SWAP)
    chip_sum = gradient_product(tokens, columns(cotangent, core)) + arrived.astype(jnp.float32)
    tokens_sibling = lax.ppermute(tokens, "core", SWAP)
    blocks = chip_sum.astype(jnp.bfloat16).reshape(4, 2, 8, 2, rows, half)
    blocks = blocks.transpose(3, 0, 1, 2, 4, 5).reshape(16, 8 * rows, half)
    plane = lax.all_to_all(blocks, PLANE, 0, 0, tiled=True)
    plane_sum = jnp.sum(plane.astype(jnp.float32), axis=0).astype(jnp.bfloat16)
    column = lax.all_to_all(plane_sum.reshape(8, rows, half), "z", 0, 0, tiled=True)
    gradient_piece = jnp.sum(column.astype(jnp.float32), axis=0)

    policy_piece = adam_update(
        gradient_piece, piece(policy), piece(anchor), piece(moment), piece(second)
    )[0].astype(jnp.bfloat16)
    column = lax.all_to_all(
        jnp.broadcast_to(policy_piece[None], (8, rows, half)), "z", 0, 0, tiled=True
    ).reshape(8 * rows, half)
    plane = lax.all_to_all(
        jnp.broadcast_to(column[None], (16, 8 * rows, half)), PLANE, 0, 0, tiled=True
    )
    policy_cols = (
        plane.reshape(2, 4, 2, 8, rows, half).transpose(1, 2, 3, 0, 4, 5).reshape(features, half)
    )

    other = lax.ppermute(gradient_piece, "core", SWAP)
    strip = jnp.where(
        core == 0,
        jnp.concatenate([gradient_piece, other], axis=1),
        jnp.concatenate([other, gradient_piece], axis=1),
    )
    other = lax.ppermute(strip, "xlo", SWAP)
    gradient = jnp.where(
        low == 0,
        jnp.concatenate([strip, other], axis=0),
        jnp.concatenate([other, strip], axis=0),
    )
    policy_next, anchor_next, moment_next, second_next = adam_update(
        gradient, policy, anchor, moment, second
    )

    readout_cols = columns(readout, core)

    def partial_margins(own):
        policy_values = jnp.dot(own, policy_cols, preferred_element_type=jnp.float32)
        frozen = jnp.dot(own, anchor_cols, preferred_element_type=jnp.float32)
        anchor_values = blend_rate * policy_values + (1.0 - blend_rate) * frozen
        gap = token_scores(policy_values, readout_cols) - token_scores(anchor_values, readout_cols)
        return jnp.sum(gap.reshape(-1, LEN), axis=1) / LEN

    parts = jnp.concatenate([partial_margins(tokens), partial_margins(tokens_sibling)])
    parts = lax.all_to_all(jnp.broadcast_to(parts[None], (256, 8)), AXES, 0, 0, tiled=True)
    parts = parts.reshape(2, 2, 64, 8)
    margins = (parts[:, :, :, :4] + parts[:, ::-1, :, 4:]).reshape(-1)
    pair_loss = pair_losses(margins, pair_index, noisy_flags)
    return (policy_next, anchor_next, moment_next, second_next, pair_loss)


def solution(mesh):
    fine = Mesh(mesh.devices.reshape(2, 2, 4, 2, 8), AXES)
    everywhere = AXES
    owners = ("y", "xhi", "z")
    placed = (
        P(everywhere, None),
        P(everywhere, None),
        P(owners, None),
        P(owners, None),
        P(owners, None),
        P(owners, None),
        P(),
        P(everywhere, None),
        P(everywhere),
    )
    return jax.shard_map(
        shards,
        mesh=fine,
        in_specs=placed,
        out_specs=(
            P(owners, None),
            P(owners, None),
            P(owners, None),
            P(owners, None),
            P(everywhere),
        ),
        check_vma=False,
    )
```

```python
import jax
import jax.numpy as jnp
from jax import lax
from jax.experimental import pallas as pl
from jax.experimental.pallas import tpu as pltpu
from jax.sharding import Mesh
from jax.sharding import PartitionSpec as P

LEN = 192


beta_one = 0.9
beta_two = 0.95
step_count = 20
learn_rate = 0.003
adam_epsilon = 1e-08
blend_rate = 0.6
smoothing = 0.1

AXES = ("xlo", "core", "y", "xhi", "z")
PLANE = ("xlo", "y", "xhi")
SWAP = ((0, 1), (1, 0))


def adam_update(gradient, policy, anchor, moment, second):
    moment_new = beta_one * moment + (1.0 - beta_one) * gradient
    second_new = beta_two * second + (1.0 - beta_two) * gradient * gradient
    correct_one = 1.0 - beta_one**step_count
    correct_two = 1.0 - beta_two**step_count
    policy_new = policy - learn_rate * (moment_new / correct_one) / (
        jnp.sqrt(second_new / correct_two) + adam_epsilon
    )
    anchor_new = blend_rate * policy_new + (1.0 - blend_rate) * anchor
    return (policy_new, anchor_new, moment_new, second_new)


def pair_losses(margins, pair_index, noisy_flags):
    sequence_index = jnp.arange(margins.shape[0], dtype=jnp.int32)
    chosen = jnp.sum(
        jnp.where(pair_index[:, 0:1] == sequence_index[None, :], margins[None, :], 0.0), axis=1
    )
    rejected = jnp.sum(
        jnp.where(pair_index[:, 1:2] == sequence_index[None, :], margins[None, :], 0.0), axis=1
    )
    margin_gap = chosen - rejected
    logit_value = jnp.where(noisy_flags == 1, -margin_gap, margin_gap)
    return -(1.0 - smoothing) * jax.nn.log_sigmoid(logit_value) - smoothing * jax.nn.log_sigmoid(
        -logit_value
    )


VMEM = 56 << 20


def gradient_kernel(core, cotangent, tokens, out, turned):
    @pl.when(pl.program_id(0) == 0)
    def _():
        turned[...] = cotangent[...].T

    product = jnp.dot(turned[...], tokens[...], preferred_element_type=jnp.float32)
    quarter = product.shape[0] // 2
    out[0, 0] = product[:quarter].astype(out.dtype)
    out[1, 0] = product[quarter:].astype(out.dtype)


def gradient_blocks(which, cotangent, tokens, dtype):
    count, features = tokens.shape
    half = cotangent.shape[1] // 2
    width = features // 8
    return pl.pallas_call(
        gradient_kernel,
        grid_spec=pltpu.PrefetchScalarGridSpec(
            num_scalar_prefetch=1,
            grid=(8,),
            in_specs=[
                pl.BlockSpec((count, half), lambda i, core: (0, core[0])),
                pl.BlockSpec((count, width), lambda i, core: (0, i)),
            ],
            out_specs=pl.BlockSpec((2, 1, half // 2, width), lambda i, core: (0, i, 0, 0)),
            scratch_shapes=[pltpu.VMEM((half, count), jnp.bfloat16)],
        ),
        out_shape=jax.ShapeDtypeStruct((2, 8, half // 2, width), dtype),
        cost_estimate=pl.CostEstimate(
            flops=2 * count * features * half, bytes_accessed=10 << 20, transcendentals=0
        ),
        compiler_params=pltpu.CompilerParams(vmem_limit_bytes=VMEM),
        name="gradient_blocks",
    )(which, cotangent, tokens)


def select_rows(tokens, sibling):
    return jnp.where(pl.program_id(0) < 2, tokens[...], sibling[...])


def weigh(tokens, sibling, halves, joined):
    quarter = halves.shape[-1]

    @pl.when(pl.program_id(0) == 0)
    def _():
        joined[:, :quarter] = halves[0]
        joined[:, quarter:] = halves[1]

    return jnp.dot(
        select_rows(tokens, sibling), joined[...], preferred_element_type=jnp.float32
    )


def frozen_kernel(place, tokens, sibling, here, left, right, far_left, far_right, out, joined):
    strips, rows, quarter = here.shape

    @pl.when(pl.program_id(0) == 0)
    def _():
        for shift, ref, first in (
            (0, here, 0), (3, left, 0), (1, right, 0), (2, far_left, 0), (2, far_right, strips // 2)
        ):
            chip = (place[0] + shift) % 4
            lanes = pl.ds(pl.multiple_of((chip % 2) * quarter, quarter), quarter)
            for at in range(ref.shape[0]):
                joined[(first + at) * 2 + chip // 2, :, lanes] = ref[at]

    weights = joined[...].reshape(joined.shape[0] * rows, 2 * quarter)
    out[...] = jnp.dot(select_rows(tokens, sibling), weights, preferred_element_type=jnp.float32)


def log_sigmoid(values):
    return jnp.minimum(values, 0.0) - jnp.log(1.0 + jnp.exp(-jnp.abs(values)))


def score_kernel(tokens, sibling, halves, frozen, readout, out, joined):
    policy_values = weigh(tokens, sibling, halves, joined)
    anchor_values = blend_rate * policy_values + (1.0 - blend_rate) * frozen[...]
    weights = readout[...]
    gap = log_sigmoid(policy_values * weights) - log_sigmoid(anchor_values * weights)
    for at in range(out.shape[1]):
        out[0, at] = jnp.sum(gap[at * LEN : (at + 1) * LEN], axis=0)


def token_specs(count, features):
    rows = count // 2
    return [
        pl.BlockSpec((rows, features), lambda i, *_: (jnp.minimum(i, 1), 0)),
        pl.BlockSpec((rows, features), lambda i, *_: (jnp.maximum(i - 2, 0), 0)),
    ]


def frozen_values(place, tokens, sibling, strips):
    count, features = tokens.shape
    width = 2 * strips[0].shape[-1]
    return pl.pallas_call(
        frozen_kernel,
        grid_spec=pltpu.PrefetchScalarGridSpec(
            num_scalar_prefetch=1,
            grid=(4,),
            in_specs=token_specs(count, features)
            + [pl.BlockSpec(strip.shape, lambda i, *_: (0, 0, 0)) for strip in strips],
            out_specs=pl.BlockSpec((count // 2, width), lambda i, *_: (i, 0)),
            scratch_shapes=[pltpu.VMEM((8, features // 8, width), jnp.bfloat16)],
        ),
        out_shape=jax.ShapeDtypeStruct((2 * count, width), jnp.float32),
        cost_estimate=pl.CostEstimate(
            flops=4 * count * features * width, bytes_accessed=16 << 20, transcendentals=0
        ),
        compiler_params=pltpu.CompilerParams(vmem_limit_bytes=VMEM),
        name="frozen_values",
    )(place, tokens, sibling, *strips)


def score_sums(tokens, sibling, halves, frozen, readout):
    count, features = tokens.shape
    width = 2 * halves.shape[-1]
    each = count // 2 // LEN
    return pl.pallas_call(
        score_kernel,
        grid=(4,),
        in_specs=token_specs(count, features)
        + [
            pl.BlockSpec(halves.shape, lambda i: (0, 0, 0)),
            pl.BlockSpec((count // 2, width), lambda i: (i, 0)),
            pl.BlockSpec((1, width), lambda i: (0, 0)),
        ],
        out_specs=pl.BlockSpec((1, each, width), lambda i: (i, 0, 0)),
        out_shape=jax.ShapeDtypeStruct((4, each, width), jnp.float32),
        scratch_shapes=[pltpu.VMEM((features, width), jnp.bfloat16)],
        cost_estimate=pl.CostEstimate(
            flops=4 * count * features * width, bytes_accessed=16 << 20, transcendentals=0
        ),
        compiler_params=pltpu.CompilerParams(vmem_limit_bytes=VMEM),
        name="score_sums",
    )(tokens, sibling, halves, frozen, readout)


def plane_sum_kernel(blocks, out):
    total = blocks[0].astype(jnp.float32)
    for at in range(1, blocks.shape[0]):
        total = total + blocks[at].astype(jnp.float32)
    out[...] = total.T.astype(out.dtype)


def plane_sum(blocks):
    _, channels, features = blocks.shape
    return pl.pallas_call(
        plane_sum_kernel,
        out_shape=jax.ShapeDtypeStruct((features, channels), jnp.bfloat16),
        compiler_params=pltpu.CompilerParams(vmem_limit_bytes=16 << 20),
        name="plane_sum",
    )(blocks)


def to_plane(blocks):
    return lax.all_to_all(blocks, PLANE, 0, 0, tiled=True)


def turn(block, shift):
    def index(x):
        return (x % 2) * 2 + x // 2

    return lax.ppermute(
        block, ("xlo", "xhi"), [(index(x), index((x + shift) % 4)) for x in range(4)]
    )


def along_z(blocks):
    return lax.all_to_all(blocks, "z", 0, 0, tiled=True)


def shards(tokens, cotangent, policy, anchor, moment, second, readout, pair_index, noisy_flags):
    core = lax.axis_index("core")
    low = lax.axis_index("xlo")
    high = lax.axis_index("xhi")
    rows, channels = policy.shape
    half, quarter = channels // 2, channels // 4
    features = tokens.shape[1]

    def piece(array):
        return lax.dynamic_slice_in_dim(array, (core * 2 + low) * quarter, quarter, axis=1)

    def spread_z(block):
        return along_z(jnp.broadcast_to(block[None], (8, rows, quarter))).reshape(8 * rows, quarter)

    def copies(column):
        return jnp.broadcast_to(column[None], (16,) + column.shape)

    def joined_halves(plane):
        return plane.reshape(2, features, quarter)

    strips = lax.all_to_all(
        jnp.broadcast_to(piece(anchor).astype(jnp.bfloat16)[None], (32, rows, quarter)),
        ("y", "z"),
        0,
        0,
        tiled=True,
    ).reshape(4, 8 * rows, quarter)

    sent = gradient_blocks((1 - core)[None], cotangent, tokens, jnp.bfloat16)
    arrived = lax.ppermute(sent, "core", SWAP)
    own = gradient_blocks(core[None], cotangent, tokens, jnp.float32)
    blocks = (own + arrived.astype(jnp.float32)).astype(jnp.bfloat16)
    tokens_out, blocks = lax.optimization_barrier((tokens, blocks))
    sibling = lax.ppermute(tokens_out, "core", SWAP)
    plane = to_plane(blocks.reshape(16, quarter, 8 * rows))
    plane, strips = lax.optimization_barrier((plane, strips))
    left, right = turn(strips, 1), turn(strips, -1)
    column = along_z(plane_sum(plane).reshape(8, rows, quarter))
    gradient_piece = jnp.sum(column.astype(jnp.float32), axis=0)

    gradient_piece, left, right = lax.optimization_barrier((gradient_piece, left, right))
    far_left, far_right = turn(left[:2], 1), turn(right[2:], -1)
    policy_piece = adam_update(
        gradient_piece, piece(policy), piece(anchor), piece(moment), piece(second)
    )[0].astype(jnp.bfloat16)
    policy_copies, far_left, far_right = lax.optimization_barrier(
        (copies(spread_z(policy_piece)), far_left, far_right)
    )
    policy_plane = to_plane(policy_copies)
    frozen = frozen_values(
        (high * 2 + low)[None], tokens, sibling, (strips, left, right, far_left, far_right)
    )

    other = lax.ppermute(gradient_piece, "xlo", SWAP)
    strip = jnp.where(
        low == 0,
        jnp.concatenate([gradient_piece, other], axis=1),
        jnp.concatenate([other, gradient_piece], axis=1),
    )
    other = lax.ppermute(strip, "core", SWAP)
    gradient = jnp.where(
        core == 0,
        jnp.concatenate([strip, other], axis=1),
        jnp.concatenate([other, strip], axis=1),
    )
    policy_next, anchor_next, moment_next, second_next = adam_update(
        gradient, policy, anchor, moment, second
    )

    readout_cols = lax.dynamic_slice_in_dim(readout, core * half, half)[None]
    sums = score_sums(tokens, sibling, joined_halves(policy_plane), frozen, readout_cols)
    parts = jnp.sum(sums, axis=2).reshape(-1) / LEN
    parts = lax.all_to_all(jnp.broadcast_to(parts[None], (256, 8)), AXES, 0, 0, tiled=True)
    parts = parts.reshape(2, 2, 64, 8)
    margins = (parts[:, :, :, :4] + parts[:, ::-1, :, 4:]).reshape(-1)
    pair_loss = pair_losses(margins, pair_index, noisy_flags)
    return (policy_next, anchor_next, moment_next, second_next, pair_loss)


def solution(mesh):
    fine = Mesh(mesh.devices.reshape(2, 2, 4, 2, 8), AXES)
    everywhere = AXES
    owners = ("y", "xhi", "z")
    placed = (
        P(everywhere, None),
        P(everywhere, None),
        P(owners, None),
        P(owners, None),
        P(owners, None),
        P(owners, None),
        P(),
        P(everywhere, None),
        P(everywhere),
    )
    return jax.shard_map(
        shards,
        mesh=fine,
        in_specs=placed,
        out_specs=(
            P(owners, None),
            P(owners, None),
            P(owners, None),
            P(owners, None),
            P(everywhere),
        ),
        check_vma=False,
    )
```

```python
import jax
import jax.numpy as jnp
from jax import lax
from jax.experimental import pallas as pl
from jax.experimental.pallas import tpu as pltpu
from jax.sharding import Mesh
from jax.sharding import PartitionSpec as P

LEN = 192


beta_one = 0.9
beta_two = 0.95
step_count = 20
learn_rate = 0.003
adam_epsilon = 1e-08
blend_rate = 0.6
smoothing = 0.1

AXES = ("xlo", "core", "y", "xhi", "z")
PLANE = ("xlo", "y", "xhi")
SWAP = ((0, 1), (1, 0))


def adam_update(gradient, policy, anchor, moment, second):
    moment_new = beta_one * moment + (1.0 - beta_one) * gradient
    second_new = beta_two * second + (1.0 - beta_two) * gradient * gradient
    correct_one = 1.0 - beta_one**step_count
    correct_two = 1.0 - beta_two**step_count
    policy_new = policy - learn_rate * (moment_new / correct_one) / (
        jnp.sqrt(second_new / correct_two) + adam_epsilon
    )
    anchor_new = blend_rate * policy_new + (1.0 - blend_rate) * anchor
    return (policy_new, anchor_new, moment_new, second_new)


def pair_losses(margins, pair_index, noisy_flags):
    sequence_index = jnp.arange(margins.shape[0], dtype=jnp.int32)
    chosen = jnp.sum(
        jnp.where(pair_index[:, 0:1] == sequence_index[None, :], margins[None, :], 0.0), axis=1
    )
    rejected = jnp.sum(
        jnp.where(pair_index[:, 1:2] == sequence_index[None, :], margins[None, :], 0.0), axis=1
    )
    margin_gap = chosen - rejected
    logit_value = jnp.where(noisy_flags == 1, -margin_gap, margin_gap)
    return -(1.0 - smoothing) * jax.nn.log_sigmoid(logit_value) - smoothing * jax.nn.log_sigmoid(
        -logit_value
    )


VMEM = 32 << 20
VMEM_GRADIENT = 32 << 20
VMEM_SCORE = 32 << 20


def gradient_kernel(core, cotangent, tokens, sent, own, turned):
    half = cotangent.shape[1] // 2
    quarter = half // 2

    @pl.when(pl.program_id(0) == 0)
    def _():
        away = pl.multiple_of((1 - core[0]) * half, half)
        here = pl.multiple_of(core[0] * half, half)
        turned[:half] = cotangent[:, pl.ds(away, half)].T
        turned[half:] = cotangent[:, pl.ds(here, half)].T

    product = jnp.dot(turned[...], tokens[...], preferred_element_type=jnp.float32)
    sent[0, 0] = product[:quarter].astype(sent.dtype)
    sent[1, 0] = product[quarter:half].astype(sent.dtype)
    own[0, 0] = product[half : half + quarter].astype(own.dtype)
    own[1, 0] = product[half + quarter :].astype(own.dtype)


def gradient_blocks(core, cotangent, tokens):
    count, features = tokens.shape
    channels = cotangent.shape[1]
    quarter = channels // 4
    width = features // 8
    block = pl.BlockSpec((2, 1, quarter, width), lambda i, core: (0, i, 0, 0))
    return pl.pallas_call(
        gradient_kernel,
        grid_spec=pltpu.PrefetchScalarGridSpec(
            num_scalar_prefetch=1,
            grid=(8,),
            in_specs=[
                pl.BlockSpec((count, channels), lambda i, core: (0, 0)),
                pl.BlockSpec((count, width), lambda i, core: (0, i)),
            ],
            out_specs=[block, block],
            scratch_shapes=[pltpu.VMEM((channels, count), jnp.bfloat16)],
        ),
        out_shape=[
            jax.ShapeDtypeStruct((2, 8, quarter, width), jnp.bfloat16),
            jax.ShapeDtypeStruct((2, 8, quarter, width), jnp.bfloat16),
        ],
        cost_estimate=pl.CostEstimate(
            flops=2 * count * features * channels, bytes_accessed=12 << 20, transcendentals=0
        ),
        compiler_params=pltpu.CompilerParams(vmem_limit_bytes=VMEM_GRADIENT),
        name="gradient_blocks",
    )(core, cotangent, tokens)


def frozen_kernel(place, tokens, sibling, here, left, right, far_left, far_right, out, joined):
    strips, rows, quarter = here.shape

    @pl.when(pl.program_id(0) == 0)
    def _():
        for shift, ref, first in (
            (0, here, 0), (3, left, 0), (1, right, 0), (2, far_left, 0), (2, far_right, strips // 2)
        ):
            chip = (place[0] + shift) % 4
            lanes = pl.ds(pl.multiple_of((chip % 2) * quarter, quarter), quarter)
            for at in range(ref.shape[0]):
                joined[(first + at) * 2 + chip // 2, :, lanes] = ref[at]

    for ref, turn_of in ((tokens, pl.program_id(0) < 2), (sibling, pl.program_id(0) >= 2)):

        @pl.when(turn_of)
        def _():
            weights = joined[...].reshape(joined.shape[0] * rows, 2 * quarter)
            out[...] = jnp.dot(ref[...], weights, preferred_element_type=jnp.float32)


def sigmoid_sums(values):
    rows = values.reshape(LEN // 8, 8, values.shape[1])
    lows = jnp.minimum(rows, 0.0)
    factors = 1.0 + jnp.exp(-jnp.abs(rows))
    low_sum, product = lows[0], factors[0]
    for step in range(1, LEN // 8):
        low_sum = low_sum + lows[step]
        product = product * factors[step]
    return low_sum - jnp.log(product)


def score_kernel(tokens, sibling, halves, frozen, readout, out, joined, held, sems):
    quarter = halves.shape[-1]
    count = tokens.shape[0]
    loads = [
        pltpu.make_async_copy(
            source.at[pl.ds(first, LEN)], held.at[pl.ds(base + first, LEN)], sems.at[at]
        )
        for at, (source, base, first) in enumerate(
            (source, base, first)
            for source, base in ((tokens, 0), (sibling, count))
            for first in range(0, count, LEN)
        )
    ]
    for load in loads:
        load.start()
    joined[:, :quarter] = halves[0]
    joined[:, quarter:] = halves[1]
    scale = readout[...]
    lane = lax.broadcasted_iota(jnp.int32, out.shape, 2)
    parts = jnp.zeros(out.shape, jnp.float32)
    for sequence, load in enumerate(loads):
        load.wait()
        rows = slice(sequence * LEN, (sequence + 1) * LEN)
        values = jnp.dot(held[rows], joined[...], preferred_element_type=jnp.float32)
        blended = blend_rate * values + (1.0 - blend_rate) * frozen[rows]
        gap = sigmoid_sums(values * scale) - sigmoid_sums(blended * scale)
        parts = jnp.where(lane == sequence, jnp.sum(gap) / LEN, parts)
    out[...] = parts


def token_specs(count, features):
    rows = count // 2
    return [
        pl.BlockSpec((rows, features), lambda i, *_: (jnp.minimum(i, 1), 0)),
        pl.BlockSpec((rows, features), lambda i, *_: (jnp.maximum(i - 2, 0), 0)),
    ]


def frozen_values(place, tokens, sibling, strips):
    count, features = tokens.shape
    width = 2 * strips[0].shape[-1]
    return pl.pallas_call(
        frozen_kernel,
        grid_spec=pltpu.PrefetchScalarGridSpec(
            num_scalar_prefetch=1,
            grid=(4,),
            in_specs=token_specs(count, features)
            + [pl.BlockSpec(strip.shape, lambda i, *_: (0, 0, 0)) for strip in strips],
            out_specs=pl.BlockSpec((count // 2, width), lambda i, *_: (i, 0)),
            scratch_shapes=[pltpu.VMEM((8, features // 8, width), jnp.bfloat16)],
        ),
        out_shape=jax.ShapeDtypeStruct((2 * count, width), jnp.float32),
        cost_estimate=pl.CostEstimate(
            flops=4 * count * features * width, bytes_accessed=16 << 20, transcendentals=0
        ),
        compiler_params=pltpu.CompilerParams(vmem_limit_bytes=VMEM),
        name="frozen_values",
    )(place, tokens, sibling, *strips)


def score_sums(tokens, sibling, halves, frozen, readout):
    count, features = tokens.shape
    width = 2 * halves.shape[-1]
    return pl.pallas_call(
        score_kernel,
        out_shape=jax.ShapeDtypeStruct((256, 1, 128), jnp.float32),
        in_specs=[pl.BlockSpec(memory_space=pl.ANY)] * 2
        + [pl.BlockSpec(memory_space=pltpu.VMEM)] * 3,
        scratch_shapes=[
            pltpu.VMEM((features, width), jnp.bfloat16),
            pltpu.VMEM((2 * count, features), tokens.dtype),
            pltpu.SemaphoreType.DMA((2 * count // LEN,)),
        ],
        cost_estimate=pl.CostEstimate(
            flops=4 * count * features * width, bytes_accessed=16 << 20, transcendentals=0
        ),
        compiler_params=pltpu.CompilerParams(vmem_limit_bytes=VMEM_SCORE),
        name="score_sums",
    )(tokens, sibling, halves, frozen, readout)


def plane_sum_kernel(blocks, out):
    total = blocks[0].astype(jnp.float32)
    for at in range(1, blocks.shape[0]):
        total = total + blocks[at].astype(jnp.float32)
    out[...] = total.T.astype(out.dtype)


def plane_sum(blocks):
    _, channels, features = blocks.shape
    return pl.pallas_call(
        plane_sum_kernel,
        out_shape=jax.ShapeDtypeStruct((features, channels), jnp.bfloat16),
        compiler_params=pltpu.CompilerParams(vmem_limit_bytes=16 << 20),
        name="plane_sum",
    )(blocks)


def to_plane(blocks):
    return lax.all_to_all(blocks, PLANE, 0, 0, tiled=True)


def turn(block, shift):
    def index(x):
        return (x % 2) * 2 + x // 2

    return lax.ppermute(
        block, ("xlo", "xhi"), [(index(x), index((x + shift) % 4)) for x in range(4)]
    )


def along_z(blocks):
    return lax.all_to_all(blocks, "z", 0, 0, tiled=True)


def shards(tokens, cotangent, policy, anchor, moment, second, readout, pair_index, noisy_flags):
    core = lax.axis_index("core")
    low = lax.axis_index("xlo")
    high = lax.axis_index("xhi")
    rows, channels = policy.shape
    half, quarter = channels // 2, channels // 4
    features = tokens.shape[1]

    def piece(array):
        return lax.dynamic_slice_in_dim(array, (core * 2 + low) * quarter, quarter, axis=1)

    def spread_z(block):
        return along_z(jnp.broadcast_to(block[None], (8, rows, quarter))).reshape(8 * rows, quarter)

    def copies(column):
        return jnp.broadcast_to(column[None], (16,) + column.shape)

    def joined_halves(plane):
        return plane.reshape(2, features, quarter)

    anchor_copies = jnp.broadcast_to(piece(anchor).astype(jnp.bfloat16)[None], (32, rows, quarter))
    anchor_copies, cotangent = lax.optimization_barrier((anchor_copies, cotangent))
    strips = lax.all_to_all(anchor_copies, ("y", "z"), 0, 0, tiled=True)
    strips = strips.reshape(4, 8 * rows, quarter)

    sent, own = gradient_blocks(core[None], cotangent, tokens)
    sent, strips = lax.optimization_barrier((sent, strips))
    arrived = lax.ppermute(sent, "core", SWAP)
    blocks = own.astype(jnp.float32) + arrived.astype(jnp.float32)
    blocks = blocks.astype(jnp.bfloat16)
    plane = to_plane(blocks.reshape(16, quarter, 8 * rows))
    plane, strips, tokens = lax.optimization_barrier((plane, strips, tokens))
    sibling = lax.ppermute(tokens, "core", SWAP)
    left, right = turn(strips, 1), turn(strips, -1)
    column = along_z(plane_sum(plane).reshape(8, rows, quarter))
    gradient_piece = jnp.sum(column.astype(jnp.float32), axis=0)

    gradient_piece, left, right = lax.optimization_barrier((gradient_piece, left, right))
    far_left, far_right = turn(left[:2], 1), turn(right[2:], -1)
    policy_piece = adam_update(
        gradient_piece, piece(policy), piece(anchor), piece(moment), piece(second)
    )[0].astype(jnp.bfloat16)
    other = lax.ppermute(gradient_piece, "xlo", SWAP)
    policy_copies, far_left, far_right, sibling, other = lax.optimization_barrier(
        (copies(spread_z(policy_piece)), far_left, far_right, sibling, other)
    )
    policy_plane = to_plane(policy_copies)
    frozen = frozen_values(
        (high * 2 + low)[None], tokens, sibling, (strips, left, right, far_left, far_right)
    )

    strip = jnp.where(
        low == 0,
        jnp.concatenate([gradient_piece, other], axis=1),
        jnp.concatenate([other, gradient_piece], axis=1),
    )
    other = lax.ppermute(strip, "core", SWAP)
    gradient = jnp.where(
        core == 0,
        jnp.concatenate([strip, other], axis=1),
        jnp.concatenate([other, strip], axis=1),
    )
    policy_next, anchor_next, moment_next, second_next = adam_update(
        gradient, policy, anchor, moment, second
    )

    readout_cols = lax.dynamic_slice_in_dim(readout, core * half, half)[None]
    parts = score_sums(tokens, sibling, joined_halves(policy_plane), frozen, readout_cols)
    parts = lax.all_to_all(parts, AXES, 0, 0, tiled=True)
    parts = parts.reshape(2, 2, 64, 128)
    margins = (parts[:, :, :, :4] + parts[:, ::-1, :, 4:8]).reshape(-1)
    pair_loss = pair_losses(margins, pair_index, noisy_flags)
    return (policy_next, anchor_next, moment_next, second_next, pair_loss)


def solution(mesh):
    fine = Mesh(mesh.devices.reshape(2, 2, 4, 2, 8), AXES)
    everywhere = AXES
    owners = ("y", "xhi", "z")
    placed = (
        P(everywhere, None),
        P(everywhere, None),
        P(owners, None),
        P(owners, None),
        P(owners, None),
        P(owners, None),
        P(),
        P(everywhere, None),
        P(everywhere),
    )
    return jax.shard_map(
        shards,
        mesh=fine,
        in_specs=placed,
        out_specs=(
            P(owners, None),
            P(owners, None),
            P(owners, None),
            P(owners, None),
            P(everywhere),
        ),
        check_vma=False,
    )
```

```python
import jax
import jax.numpy as jnp
from jax import lax
from jax.experimental import pallas as pl
from jax.experimental.pallas import tpu as pltpu
from jax.sharding import Mesh
from jax.sharding import PartitionSpec as P

LEN = 192


beta_one = 0.9
beta_two = 0.95
step_count = 20
learn_rate = 0.003
adam_epsilon = 1e-08
blend_rate = 0.6
smoothing = 0.1

AXES = ("xlo", "core", "y", "xhi", "z")
PLANE = ("xlo", "y", "xhi")
SWAP = ((0, 1), (1, 0))


def adam_update(gradient, policy, anchor, moment, second):
    moment_new = beta_one * moment + (1.0 - beta_one) * gradient
    second_new = beta_two * second + (1.0 - beta_two) * gradient * gradient
    correct_one = 1.0 - beta_one**step_count
    correct_two = 1.0 - beta_two**step_count
    policy_new = policy - learn_rate * (moment_new / correct_one) / (
        jnp.sqrt(second_new / correct_two) + adam_epsilon
    )
    anchor_new = blend_rate * policy_new + (1.0 - blend_rate) * anchor
    return (policy_new, anchor_new, moment_new, second_new)


def pair_losses(margins, pair_index, noisy_flags):
    sequence_index = jnp.arange(margins.shape[0], dtype=jnp.int32)
    chosen = jnp.sum(
        jnp.where(pair_index[:, 0:1] == sequence_index[None, :], margins[None, :], 0.0), axis=1
    )
    rejected = jnp.sum(
        jnp.where(pair_index[:, 1:2] == sequence_index[None, :], margins[None, :], 0.0), axis=1
    )
    margin_gap = chosen - rejected
    logit_value = jnp.where(noisy_flags == 1, -margin_gap, margin_gap)
    return -(1.0 - smoothing) * jax.nn.log_sigmoid(logit_value) - smoothing * jax.nn.log_sigmoid(
        -logit_value
    )


VMEM = 32 << 20
VMEM_GRADIENT = 32 << 20
VMEM_SCORE = 32 << 20


def in_hbm(array):
    return pltpu.with_memory_space_constraint(array, pltpu.HBM)


def gradient_kernel(place, cotangent, tokens, anchor, sent, own, message, held, turned, sems):
    channels = held.shape[1]
    half, quarter = channels // 2, channels // 4
    width = sent.shape[3]
    core = place[0]
    halves = [
        pltpu.make_async_copy(
            cotangent.at[:, pl.ds(pl.multiple_of(which * half, half), half)],
            held.at[:, pl.ds(at * half, half)],
            sems.at[at],
        )
        for at, which in enumerate((1 - core, core))
    ]
    blocks = [
        pltpu.make_async_copy(
            tokens.at[:, pl.ds(at * width, width)],
            turned.at[:, pl.ds(at * width, width)],
            sems.at[2 + at],
        )
        for at in range(8)
    ]
    for load in halves + blocks:
        load.start()
    lanes = pl.ds(pl.multiple_of(place[1] * quarter, quarter), quarter)
    piece = anchor[:, lanes].astype(message.dtype)
    for at in range(message.shape[0]):
        message[at] = piece
    for load in halves:
        load.wait()
    for at, load in enumerate(blocks):
        load.wait()
        product = lax.dot_general(
            held[...],
            turned[:, at * width : (at + 1) * width],
            (((0,), (0,)), ((), ())),
            preferred_element_type=jnp.float32,
        ).astype(sent.dtype)
        sent[0, at] = product[:quarter]
        sent[1, at] = product[quarter:half]
        own[0, at] = product[half : half + quarter]
        own[1, at] = product[half + quarter :]


def gradient_blocks(place, cotangent, tokens, anchor):
    count, features = tokens.shape
    channels = cotangent.shape[1]
    quarter = channels // 4
    width = features // 8
    block = pltpu.VMEM((2, 8, quarter, width), jnp.bfloat16)
    return pl.pallas_call(
        gradient_kernel,
        in_specs=[
            pl.BlockSpec(memory_space=pltpu.SMEM),
            pl.BlockSpec(memory_space=pltpu.HBM),
            pl.BlockSpec(memory_space=pltpu.HBM),
            pl.BlockSpec(memory_space=pltpu.VMEM),
        ],
        out_specs=[pl.BlockSpec(memory_space=pltpu.VMEM)] * 3,
        out_shape=[block, block, jax.ShapeDtypeStruct((32, anchor.shape[0], quarter), jnp.bfloat16)],
        scratch_shapes=[
            pltpu.VMEM(cotangent.shape, cotangent.dtype),
            pltpu.VMEM(tokens.shape, tokens.dtype),
            pltpu.SemaphoreType.DMA((10,)),
        ],
        cost_estimate=pl.CostEstimate(
            flops=2 * count * features * channels, bytes_accessed=12 << 20, transcendentals=0
        ),
        compiler_params=pltpu.CompilerParams(vmem_limit_bytes=VMEM_GRADIENT),
        name="gradient_blocks",
    )(place, in_hbm(cotangent), in_hbm(tokens), anchor)


def frozen_kernel(place, tokens, sibling, here, left, right, far_left, far_right, out, joined):
    strips, rows, quarter = here.shape

    @pl.when(pl.program_id(0) == 0)
    def _():
        for shift, ref, first in (
            (0, here, 0), (3, left, 0), (1, right, 0), (2, far_left, 0), (2, far_right, strips // 2)
        ):
            chip = (place[0] + shift) % 4
            lanes = pl.ds(pl.multiple_of((chip % 2) * quarter, quarter), quarter)
            for at in range(ref.shape[0]):
                joined[(first + at) * 2 + chip // 2, :, lanes] = ref[at]

    for ref, turn_of in ((tokens, pl.program_id(0) < 2), (sibling, pl.program_id(0) >= 2)):

        @pl.when(turn_of)
        def _():
            weights = joined[...].reshape(joined.shape[0] * rows, 2 * quarter)
            out[...] = jnp.dot(ref[...], weights, preferred_element_type=jnp.float32)


def sigmoid_sums(values):
    rows = values.reshape(LEN // 8, 8, values.shape[1])
    lows = jnp.minimum(rows, 0.0)
    factors = 1.0 + jnp.exp(-jnp.abs(rows))
    low_sum, product = lows[0], factors[0]
    for step in range(1, LEN // 8):
        low_sum = low_sum + lows[step]
        product = product * factors[step]
    return low_sum - jnp.log(product)


def score_kernel(tokens, sibling, halves, frozen, readout, out, joined, held, still, sems):
    quarter = halves.shape[-1]
    count = tokens.shape[0]
    sizes = (2 * LEN, 2 * LEN, 2 * LEN, LEN, LEN)
    loads, at = [], 0
    for step, size in enumerate(sizes):
        source, first = (tokens, at) if at < count else (sibling, at - count)
        span = pl.ds(at, size)
        loads.append(
            (
                pltpu.make_async_copy(
                    source.at[pl.ds(first, size)], held.at[span], sems.at[2 * step]
                ),
                pltpu.make_async_copy(frozen.at[span], still.at[span], sems.at[2 * step + 1]),
            )
        )
        at += size
    for pair in loads:
        for load in pair:
            load.start()
    joined[:, :quarter] = halves[0]
    joined[:, quarter:] = halves[1]
    scale = readout[...]
    lane = lax.broadcasted_iota(jnp.int32, (1, 128), 1)
    parts = jnp.zeros((1, 128), jnp.float32)
    at = 0
    for pair, size in zip(loads, sizes):
        for load in pair:
            load.wait()
        values = jnp.dot(held[at : at + size], joined[...], preferred_element_type=jnp.float32)
        blended = blend_rate * values + (1.0 - blend_rate) * still[at : at + size]
        values, blended = values * scale, blended * scale
        for first in range(0, size, LEN):
            rows = slice(first, first + LEN)
            gap = sigmoid_sums(values[rows]) - sigmoid_sums(blended[rows])
            parts = jnp.where(lane == (at + first) // LEN, jnp.sum(gap) / LEN, parts)
        at += size
    out[...] = jnp.broadcast_to(parts[None], out.shape)


def token_specs(count, features):
    rows = count // 2
    return [
        pl.BlockSpec((rows, features), lambda i, *_: (jnp.minimum(i, 1), 0)),
        pl.BlockSpec((rows, features), lambda i, *_: (jnp.maximum(i - 2, 0), 0)),
    ]


def frozen_values(place, tokens, sibling, strips):
    count, features = tokens.shape
    width = 2 * strips[0].shape[-1]
    return pl.pallas_call(
        frozen_kernel,
        grid_spec=pltpu.PrefetchScalarGridSpec(
            num_scalar_prefetch=1,
            grid=(4,),
            in_specs=token_specs(count, features)
            + [pl.BlockSpec(strip.shape, lambda i, *_: (0, 0, 0)) for strip in strips],
            out_specs=pl.BlockSpec((count // 2, width), lambda i, *_: (i, 0)),
            scratch_shapes=[pltpu.VMEM((8, features // 8, width), jnp.bfloat16)],
        ),
        out_shape=jax.ShapeDtypeStruct((2 * count, width), jnp.float32),
        cost_estimate=pl.CostEstimate(
            flops=4 * count * features * width, bytes_accessed=16 << 20, transcendentals=0
        ),
        compiler_params=pltpu.CompilerParams(vmem_limit_bytes=VMEM),
        name="frozen_values",
    )(place, in_hbm(tokens), in_hbm(sibling), *strips)


def score_sums(tokens, sibling, halves, frozen, readout):
    count, features = tokens.shape
    width = 2 * halves.shape[-1]
    return pl.pallas_call(
        score_kernel,
        out_shape=jax.ShapeDtypeStruct((256, 1, 128), jnp.float32),
        in_specs=[
            pl.BlockSpec(memory_space=pltpu.HBM),
            pl.BlockSpec(memory_space=pltpu.HBM),
            pl.BlockSpec(memory_space=pltpu.VMEM),
            pl.BlockSpec(memory_space=pltpu.HBM),
            pl.BlockSpec(memory_space=pltpu.VMEM),
        ],
        scratch_shapes=[
            pltpu.VMEM((features, width), jnp.bfloat16),
            pltpu.VMEM((2 * count, features), tokens.dtype),
            pltpu.VMEM(frozen.shape, frozen.dtype),
            pltpu.SemaphoreType.DMA((10,)),
        ],
        cost_estimate=pl.CostEstimate(
            flops=4 * count * features * width, bytes_accessed=16 << 20, transcendentals=0
        ),
        compiler_params=pltpu.CompilerParams(vmem_limit_bytes=VMEM_SCORE),
        name="score_sums",
    )(in_hbm(tokens), in_hbm(sibling), halves, in_hbm(frozen), readout)


def plane_sum_kernel(blocks, out):
    total = blocks[0].astype(jnp.float32)
    for at in range(1, blocks.shape[0]):
        total = total + blocks[at].astype(jnp.float32)
    out[...] = total.T.astype(out.dtype)


def plane_sum(blocks):
    _, channels, features = blocks.shape
    return pl.pallas_call(
        plane_sum_kernel,
        out_shape=jax.ShapeDtypeStruct((features, channels), jnp.bfloat16),
        compiler_params=pltpu.CompilerParams(vmem_limit_bytes=16 << 20),
        name="plane_sum",
    )(blocks)


def to_plane(blocks):
    return lax.all_to_all(blocks, PLANE, 0, 0, tiled=True)


def turn(block, shift):
    def index(x):
        return (x % 2) * 2 + x // 2

    return lax.ppermute(
        block, ("xlo", "xhi"), [(index(x), index((x + shift) % 4)) for x in range(4)]
    )


def along_z(blocks):
    return lax.all_to_all(blocks, "z", 0, 0, tiled=True)


def shards(tokens, cotangent, policy, anchor, moment, second, readout, pair_index, noisy_flags):
    core = lax.axis_index("core")
    low = lax.axis_index("xlo")
    high = lax.axis_index("xhi")
    rows, channels = policy.shape
    half, quarter = channels // 2, channels // 4
    features = tokens.shape[1]

    def piece(array):
        return lax.dynamic_slice_in_dim(array, (core * 2 + low) * quarter, quarter, axis=1)

    def spread_z(block):
        return along_z(jnp.broadcast_to(block[None], (8, rows, quarter))).reshape(8 * rows, quarter)

    def copies(column):
        return jnp.broadcast_to(column[None], (16,) + column.shape)

    def joined_halves(plane):
        return plane.reshape(2, features, quarter)

    sent, own, anchor_copies = gradient_blocks(
        jnp.stack([core, core * 2 + low]), cotangent, tokens, anchor
    )
    arrived = lax.ppermute(sent, "core", SWAP)
    strips = lax.all_to_all(anchor_copies, ("y", "z"), 0, 0, tiled=True)
    strips = strips.reshape(4, 8 * rows, quarter)
    blocks = own.astype(jnp.float32) + arrived.astype(jnp.float32)
    blocks = blocks.astype(jnp.bfloat16)
    blocks, strips = lax.optimization_barrier((blocks, strips))
    plane = to_plane(blocks.reshape(16, quarter, 8 * rows))
    plane, strips, tokens = lax.optimization_barrier((plane, strips, tokens))
    sibling = lax.ppermute(tokens, "core", SWAP)
    left, right = turn(strips, 1), turn(strips, -1)
    column = along_z(plane_sum(plane).reshape(8, rows, quarter))
    gradient_piece = jnp.sum(column.astype(jnp.float32), axis=0)

    gradient_piece, left, right = lax.optimization_barrier((gradient_piece, left, right))
    far_left, far_right = turn(left[:2], 1), turn(right[2:], -1)
    policy_piece = adam_update(
        gradient_piece, piece(policy), piece(anchor), piece(moment), piece(second)
    )[0].astype(jnp.bfloat16)
    other = lax.ppermute(gradient_piece, "xlo", SWAP)
    policy_copies, far_left, far_right, sibling, other = lax.optimization_barrier(
        (copies(spread_z(policy_piece)), far_left, far_right, sibling, other)
    )
    policy_plane = to_plane(policy_copies)
    frozen = frozen_values(
        (high * 2 + low)[None], tokens, sibling, (strips, left, right, far_left, far_right)
    )

    strip = jnp.where(
        low == 0,
        jnp.concatenate([gradient_piece, other], axis=1),
        jnp.concatenate([other, gradient_piece], axis=1),
    )
    other = lax.ppermute(strip, "core", SWAP)
    gradient = jnp.where(
        core == 0,
        jnp.concatenate([strip, other], axis=1),
        jnp.concatenate([other, strip], axis=1),
    )
    policy_next, anchor_next, moment_next, second_next = adam_update(
        gradient, policy, anchor, moment, second
    )

    readout_cols = lax.dynamic_slice_in_dim(readout, core * half, half)[None]
    parts = score_sums(tokens, sibling, joined_halves(policy_plane), frozen, readout_cols)
    parts = lax.all_to_all(parts, AXES, 0, 0, tiled=True)
    parts = parts.reshape(2, 2, 64, 128)
    margins = (parts[:, :, :, :4] + parts[:, ::-1, :, 4:8]).reshape(-1)
    pair_loss = pair_losses(margins, pair_index, noisy_flags)
    return (policy_next, anchor_next, moment_next, second_next, pair_loss)


def solution(mesh):
    fine = Mesh(mesh.devices.reshape(2, 2, 4, 2, 8), AXES)
    everywhere = AXES
    owners = ("y", "xhi", "z")
    placed = (
        P(everywhere, None),
        P(everywhere, None),
        P(owners, None),
        P(owners, None),
        P(owners, None),
        P(owners, None),
        P(),
        P(everywhere, None),
        P(everywhere),
    )
    return jax.shard_map(
        shards,
        mesh=fine,
        in_specs=placed,
        out_specs=(
            P(owners, None),
            P(owners, None),
            P(owners, None),
            P(owners, None),
            P(everywhere),
        ),
        check_vma=False,
    )
```

```python
import jax
import jax.numpy as jnp
from jax import lax
from jax.experimental import pallas as pl
from jax.experimental.pallas import tpu as pltpu
from jax.sharding import Mesh
from jax.sharding import PartitionSpec as P

LEN = 192


beta_one = 0.9
beta_two = 0.95
step_count = 20
learn_rate = 0.003
adam_epsilon = 1e-08
blend_rate = 0.6
smoothing = 0.1

AXES = ("xlo", "core", "y", "xhi", "z")
PLANE = ("xlo", "y", "xhi")
SWAP = ((0, 1), (1, 0))


def adam_update(gradient, policy, anchor, moment, second):
    moment_new = beta_one * moment + (1.0 - beta_one) * gradient
    second_new = beta_two * second + (1.0 - beta_two) * gradient * gradient
    correct_one = 1.0 - beta_one**step_count
    correct_two = 1.0 - beta_two**step_count
    policy_new = policy - learn_rate * (moment_new / correct_one) / (
        jnp.sqrt(second_new / correct_two) + adam_epsilon
    )
    anchor_new = blend_rate * policy_new + (1.0 - blend_rate) * anchor
    return (policy_new, anchor_new, moment_new, second_new)


def pair_losses(margins, pair_index, noisy_flags):
    sequence_index = jnp.arange(margins.shape[0], dtype=jnp.int32)
    chosen = jnp.sum(
        jnp.where(pair_index[:, 0:1] == sequence_index[None, :], margins[None, :], 0.0), axis=1
    )
    rejected = jnp.sum(
        jnp.where(pair_index[:, 1:2] == sequence_index[None, :], margins[None, :], 0.0), axis=1
    )
    margin_gap = chosen - rejected
    logit_value = jnp.where(noisy_flags == 1, -margin_gap, margin_gap)
    return -(1.0 - smoothing) * jax.nn.log_sigmoid(logit_value) - smoothing * jax.nn.log_sigmoid(
        -logit_value
    )


VMEM = 32 << 20
VMEM_GRADIENT = 32 << 20
VMEM_SCORE = 32 << 20


def in_hbm(array):
    return pltpu.with_memory_space_constraint(array, pltpu.HBM)


def gradient_kernel(place, cotangent, tokens, sent, own, held, turned, sems):
    channels = held.shape[1]
    half, quarter = channels // 2, channels // 4
    width = sent.shape[3]
    core = place[0]
    halves = [
        pltpu.make_async_copy(
            cotangent.at[:, pl.ds(pl.multiple_of(which * half, half), half)],
            held.at[:, pl.ds(at * half, half)],
            sems.at[at],
        )
        for at, which in enumerate((1 - core, core))
    ]
    blocks = [
        pltpu.make_async_copy(
            tokens.at[:, pl.ds(at * width, width)],
            turned.at[:, pl.ds(at * width, width)],
            sems.at[2 + at],
        )
        for at in range(8)
    ]
    for load in halves + blocks:
        load.start()
    for load in halves:
        load.wait()
    for at, load in enumerate(blocks):
        load.wait()
        product = lax.dot_general(
            held[...],
            turned[:, at * width : (at + 1) * width],
            (((0,), (0,)), ((), ())),
            preferred_element_type=jnp.float32,
        ).astype(sent.dtype)
        sent[0, at] = product[:quarter]
        sent[1, at] = product[quarter:half]
        own[0, at] = product[half : half + quarter]
        own[1, at] = product[half + quarter :]


def gradient_blocks(place, cotangent, tokens):
    count, features = tokens.shape
    channels = cotangent.shape[1]
    quarter = channels // 4
    width = features // 8
    block = pltpu.VMEM((2, 8, quarter, width), jnp.bfloat16)
    return pl.pallas_call(
        gradient_kernel,
        in_specs=[
            pl.BlockSpec(memory_space=pltpu.SMEM),
            pl.BlockSpec(memory_space=pltpu.HBM),
            pl.BlockSpec(memory_space=pltpu.HBM),
        ],
        out_specs=[pl.BlockSpec(memory_space=pltpu.VMEM)] * 2,
        out_shape=[block, block],
        scratch_shapes=[
            pltpu.VMEM(cotangent.shape, cotangent.dtype),
            pltpu.VMEM(tokens.shape, tokens.dtype),
            pltpu.SemaphoreType.DMA((10,)),
        ],
        cost_estimate=pl.CostEstimate(
            flops=2 * count * features * channels, bytes_accessed=12 << 20, transcendentals=0
        ),
        compiler_params=pltpu.CompilerParams(vmem_limit_bytes=VMEM_GRADIENT),
        name="gradient_blocks",
    )(place, in_hbm(cotangent), in_hbm(tokens))


def frozen_kernel(place, tokens, sibling, here, left, right, far_left, far_right, out, joined):
    depth, count, rows, quarter = here.shape

    @pl.when(pl.program_id(0) == 0)
    def _():
        for shift, ref, first in (
            (0, here, 0), (3, left, 0), (1, right, 0), (2, far_left, 0), (2, far_right, depth // 2)
        ):
            chip = (place[0] + shift) % 4
            lanes = pl.ds(pl.multiple_of((chip % 2) * quarter, quarter), quarter)
            for at in range(ref.shape[0]):
                level = (place[2] + first + at) % 8
                for turn_y in range(count):
                    owner = ((place[1] + turn_y) % 4) * 16 + (chip // 2) * 8 + level
                    span = pl.ds(pl.multiple_of(owner * rows, rows), rows)
                    joined[span, lanes] = ref[at, turn_y]

    for ref, turn_of in ((tokens, pl.program_id(0) < 2), (sibling, pl.program_id(0) >= 2)):

        @pl.when(turn_of)
        def _():
            out[...] = jnp.dot(ref[...], joined[...], preferred_element_type=jnp.float32)


def sigmoid_sums(values):
    rows = values.reshape(LEN // 8, 8, values.shape[1])
    lows = jnp.minimum(rows, 0.0)
    factors = 1.0 + jnp.exp(-jnp.abs(rows))
    low_sum, product = lows[0], factors[0]
    for step in range(1, LEN // 8):
        low_sum = low_sum + lows[step]
        product = product * factors[step]
    return low_sum - jnp.log(product)


def score_kernel(tokens, sibling, halves, frozen, readout, out, joined, held, still, sems):
    quarter = halves.shape[-1]
    count = tokens.shape[0]
    sizes = (2 * LEN, 2 * LEN, 2 * LEN, LEN, LEN)
    loads, at = [], 0
    for step, size in enumerate(sizes):
        source, first = (tokens, at) if at < count else (sibling, at - count)
        span = pl.ds(at, size)
        loads.append(
            (
                pltpu.make_async_copy(
                    source.at[pl.ds(first, size)], held.at[span], sems.at[2 * step]
                ),
                pltpu.make_async_copy(frozen.at[span], still.at[span], sems.at[2 * step + 1]),
            )
        )
        at += size
    for pair in loads:
        for load in pair:
            load.start()
    joined[:, :quarter] = halves[0]
    joined[:, quarter:] = halves[1]
    scale = readout[...]
    lane = lax.broadcasted_iota(jnp.int32, (1, 128), 1)
    parts = jnp.zeros((1, 128), jnp.float32)
    at = 0
    for pair, size in zip(loads, sizes):
        for load in pair:
            load.wait()
        values = jnp.dot(held[at : at + size], joined[...], preferred_element_type=jnp.float32)
        blended = blend_rate * values + (1.0 - blend_rate) * still[at : at + size]
        values, blended = values * scale, blended * scale
        for first in range(0, size, LEN):
            rows = slice(first, first + LEN)
            gap = sigmoid_sums(values[rows]) - sigmoid_sums(blended[rows])
            parts = jnp.where(lane == (at + first) // LEN, jnp.sum(gap) / LEN, parts)
        at += size
    out[...] = jnp.broadcast_to(parts[None], out.shape)


def token_specs(count, features):
    rows = count // 2
    return [
        pl.BlockSpec((rows, features), lambda i, *_: (jnp.minimum(i, 1), 0)),
        pl.BlockSpec((rows, features), lambda i, *_: (jnp.maximum(i - 2, 0), 0)),
    ]


def frozen_values(place, tokens, sibling, strips):
    count, features = tokens.shape
    width = 2 * strips[0].shape[-1]
    return pl.pallas_call(
        frozen_kernel,
        grid_spec=pltpu.PrefetchScalarGridSpec(
            num_scalar_prefetch=1,
            grid=(4,),
            in_specs=token_specs(count, features)
            + [pl.BlockSpec(strip.shape, lambda i, *_: (0, 0, 0, 0)) for strip in strips],
            out_specs=pl.BlockSpec((count // 2, width), lambda i, *_: (i, 0)),
            scratch_shapes=[pltpu.VMEM((features, width), jnp.bfloat16)],
        ),
        out_shape=jax.ShapeDtypeStruct((2 * count, width), jnp.float32),
        cost_estimate=pl.CostEstimate(
            flops=4 * count * features * width, bytes_accessed=16 << 20, transcendentals=0
        ),
        compiler_params=pltpu.CompilerParams(vmem_limit_bytes=VMEM),
        name="frozen_values",
    )(place, in_hbm(tokens), in_hbm(sibling), *strips)


def score_sums(tokens, sibling, halves, frozen, readout):
    count, features = tokens.shape
    width = 2 * halves.shape[-1]
    return pl.pallas_call(
        score_kernel,
        out_shape=jax.ShapeDtypeStruct((256, 1, 128), jnp.float32),
        in_specs=[
            pl.BlockSpec(memory_space=pltpu.HBM),
            pl.BlockSpec(memory_space=pltpu.HBM),
            pl.BlockSpec(memory_space=pltpu.VMEM),
            pl.BlockSpec(memory_space=pltpu.HBM),
            pl.BlockSpec(memory_space=pltpu.VMEM),
        ],
        scratch_shapes=[
            pltpu.VMEM((features, width), jnp.bfloat16),
            pltpu.VMEM((2 * count, features), tokens.dtype),
            pltpu.VMEM(frozen.shape, frozen.dtype),
            pltpu.SemaphoreType.DMA((10,)),
        ],
        cost_estimate=pl.CostEstimate(
            flops=4 * count * features * width, bytes_accessed=16 << 20, transcendentals=0
        ),
        compiler_params=pltpu.CompilerParams(vmem_limit_bytes=VMEM_SCORE),
        name="score_sums",
    )(in_hbm(tokens), in_hbm(sibling), halves, in_hbm(frozen), readout)


def plane_sum_kernel(blocks, out):
    total = blocks[0].astype(jnp.float32)
    for at in range(1, blocks.shape[0]):
        total = total + blocks[at].astype(jnp.float32)
    out[...] = total.T.astype(out.dtype)


def plane_sum(blocks):
    _, channels, features = blocks.shape
    return pl.pallas_call(
        plane_sum_kernel,
        out_shape=jax.ShapeDtypeStruct((features, channels), jnp.bfloat16),
        compiler_params=pltpu.CompilerParams(vmem_limit_bytes=16 << 20),
        name="plane_sum",
    )(blocks)


def to_plane(blocks):
    return lax.all_to_all(blocks, PLANE, 0, 0, tiled=True)


def turn(block, shift):
    def index(x):
        return (x % 2) * 2 + x // 2

    return lax.ppermute(
        block, ("xlo", "xhi"), [(index(x), index((x + shift) % 4)) for x in range(4)]
    )


def shift_ring(block, axis, size, shift):
    return lax.ppermute(block, axis, [(i, (i - shift) % size) for i in range(size)])


def column_strips(piece):
    pair = jnp.stack([piece, shift_ring(piece, "y", 4, 1)])
    own = jnp.concatenate([pair, shift_ring(pair, "y", 4, 2)])[None]
    above, below = shift_ring(own, "z", 8, 1), shift_ring(own, "z", 8, -1)
    upper = shift_ring(jnp.concatenate([below, own, above]), "z", 8, 3)
    lower = shift_ring(jnp.concatenate([own, above]), "z", 8, -3)
    return jnp.concatenate([own, above, upper, lower, below])


def along_z(blocks):
    return lax.all_to_all(blocks, "z", 0, 0, tiled=True)


def shards(tokens, cotangent, policy, anchor, moment, second, readout, pair_index, noisy_flags):
    core = lax.axis_index("core")
    low = lax.axis_index("xlo")
    high = lax.axis_index("xhi")
    rows, channels = policy.shape
    half, quarter = channels // 2, channels // 4
    features = tokens.shape[1]

    def piece(array):
        return lax.dynamic_slice_in_dim(array, (core * 2 + low) * quarter, quarter, axis=1)

    def spread_z(block):
        return along_z(jnp.broadcast_to(block[None], (8, rows, quarter))).reshape(8 * rows, quarter)

    def copies(column):
        return jnp.broadcast_to(column[None], (16,) + column.shape)

    def joined_halves(plane):
        return plane.reshape(2, features, quarter)

    sent, own = gradient_blocks(core[None], cotangent, tokens)
    sent, anchor_piece = lax.optimization_barrier((sent, piece(anchor).astype(jnp.bfloat16)))
    arrived = lax.ppermute(sent, "core", SWAP)
    strips = column_strips(anchor_piece)
    blocks = own.astype(jnp.float32) + arrived.astype(jnp.float32)
    blocks = blocks.astype(jnp.bfloat16)
    plane = to_plane(blocks.reshape(16, quarter, 8 * rows))
    plane, strips, tokens = lax.optimization_barrier((plane, strips, tokens))
    sibling = lax.ppermute(tokens, "core", SWAP)
    left, right = turn(strips, 1), turn(strips, -1)
    column = along_z(plane_sum(plane).reshape(8, rows, quarter))
    gradient_piece = jnp.sum(column.astype(jnp.float32), axis=0)

    far_left, far_right = turn(left[:4], 1), turn(right[4:], -1)
    policy_piece = adam_update(
        gradient_piece, piece(policy), piece(anchor), piece(moment), piece(second)
    )[0].astype(jnp.bfloat16)
    other = lax.ppermute(gradient_piece, "xlo", SWAP)
    policy_copies, far_left, far_right, sibling, other = lax.optimization_barrier(
        (copies(spread_z(policy_piece)), far_left, far_right, sibling, other)
    )
    policy_plane = to_plane(policy_copies)
    frozen = frozen_values(
        jnp.stack([high * 2 + low, lax.axis_index("y"), lax.axis_index("z")]), tokens, sibling, (strips, left, right, far_left, far_right)
    )

    strip = jnp.where(
        low == 0,
        jnp.concatenate([gradient_piece, other], axis=1),
        jnp.concatenate([other, gradient_piece], axis=1),
    )
    other = lax.ppermute(strip, "core", SWAP)
    gradient = jnp.where(
        core == 0,
        jnp.concatenate([strip, other], axis=1),
        jnp.concatenate([other, strip], axis=1),
    )
    policy_next, anchor_next, moment_next, second_next = adam_update(
        gradient, policy, anchor, moment, second
    )

    readout_cols = lax.dynamic_slice_in_dim(readout, core * half, half)[None]
    parts = score_sums(tokens, sibling, joined_halves(policy_plane), frozen, readout_cols)
    parts = lax.all_to_all(parts, AXES, 0, 0, tiled=True)
    parts = parts.reshape(2, 2, 64, 128)
    margins = (parts[:, :, :, :4] + parts[:, ::-1, :, 4:8]).reshape(-1)
    pair_loss = pair_losses(margins, pair_index, noisy_flags)
    return (policy_next, anchor_next, moment_next, second_next, pair_loss)


def solution(mesh):
    fine = Mesh(mesh.devices.reshape(2, 2, 4, 2, 8), AXES)
    everywhere = AXES
    owners = ("y", "xhi", "z")
    placed = (
        P(everywhere, None),
        P(everywhere, None),
        P(owners, None),
        P(owners, None),
        P(owners, None),
        P(owners, None),
        P(),
        P(everywhere, None),
        P(everywhere),
    )
    return jax.shard_map(
        shards,
        mesh=fine,
        in_specs=placed,
        out_specs=(
            P(owners, None),
            P(owners, None),
            P(owners, None),
            P(owners, None),
            P(everywhere),
        ),
        check_vma=False,
    )
```

```python
import jax
import jax.numpy as jnp
from jax import lax
from jax.experimental import pallas as pl
from jax.experimental.pallas import tpu as pltpu
from jax.sharding import Mesh
from jax.sharding import PartitionSpec as P

LEN = 192


beta_one = 0.9
beta_two = 0.95
step_count = 20
learn_rate = 0.003
adam_epsilon = 1e-08
blend_rate = 0.6
smoothing = 0.1

AXES = ("xlo", "core", "y", "xhi", "z")
PLANE = ("xlo", "y", "xhi")
SWAP = ((0, 1), (1, 0))


def adam_update(gradient, policy, anchor, moment, second):
    moment_new = beta_one * moment + (1.0 - beta_one) * gradient
    second_new = beta_two * second + (1.0 - beta_two) * gradient * gradient
    correct_one = 1.0 - beta_one**step_count
    correct_two = 1.0 - beta_two**step_count
    policy_new = policy - learn_rate * (moment_new / correct_one) / (
        jnp.sqrt(second_new / correct_two) + adam_epsilon
    )
    anchor_new = blend_rate * policy_new + (1.0 - blend_rate) * anchor
    return (policy_new, anchor_new, moment_new, second_new)


def pair_losses(margins, pair_index, noisy_flags):
    sequence_index = jnp.arange(margins.shape[0], dtype=jnp.int32)
    chosen = jnp.sum(
        jnp.where(pair_index[:, 0:1] == sequence_index[None, :], margins[None, :], 0.0), axis=1
    )
    rejected = jnp.sum(
        jnp.where(pair_index[:, 1:2] == sequence_index[None, :], margins[None, :], 0.0), axis=1
    )
    margin_gap = chosen - rejected
    logit_value = jnp.where(noisy_flags == 1, -margin_gap, margin_gap)
    return -(1.0 - smoothing) * jax.nn.log_sigmoid(logit_value) - smoothing * jax.nn.log_sigmoid(
        -logit_value
    )


VMEM = 32 << 20
VMEM_GRADIENT = 32 << 20
VMEM_SCORE = 32 << 20
AHEAD = 3


def in_hbm(array):
    return pltpu.with_memory_space_constraint(array, pltpu.HBM)


def gradient_kernel(place, cotangent, tokens, sent, own, held, turned, sems):
    channels = held.shape[1]
    half, quarter = channels // 2, channels // 4
    width = sent.shape[3]
    core = place[0]
    halves = [
        pltpu.make_async_copy(
            cotangent.at[:, pl.ds(pl.multiple_of(which * half, half), half)],
            held.at[:, pl.ds(at * half, half)],
            sems.at[at],
        )
        for at, which in enumerate((1 - core, core))
    ]
    blocks = [
        pltpu.make_async_copy(
            tokens.at[:, pl.ds(at * width, width)],
            turned.at[:, pl.ds(at * width, width)],
            sems.at[2 + at],
        )
        for at in range(8)
    ]
    for load in halves + blocks[:AHEAD]:
        load.start()
    for load in halves:
        load.wait()
    for at, load in enumerate(blocks):
        load.wait()
        if at + AHEAD < len(blocks):
            blocks[at + AHEAD].start()
        product = lax.dot_general(
            held[...],
            turned[:, at * width : (at + 1) * width],
            (((0,), (0,)), ((), ())),
            preferred_element_type=jnp.float32,
        ).astype(sent.dtype)
        sent[0, at] = product[:quarter]
        sent[1, at] = product[quarter:half]
        own[0, at] = product[half : half + quarter]
        own[1, at] = product[half + quarter :]


def gradient_blocks(place, cotangent, tokens):
    count, features = tokens.shape
    channels = cotangent.shape[1]
    quarter = channels // 4
    width = features // 8
    block = pltpu.VMEM((2, 8, quarter, width), jnp.bfloat16)
    return pl.pallas_call(
        gradient_kernel,
        in_specs=[
            pl.BlockSpec(memory_space=pltpu.SMEM),
            pl.BlockSpec(memory_space=pltpu.HBM),
            pl.BlockSpec(memory_space=pltpu.HBM),
        ],
        out_specs=[pl.BlockSpec(memory_space=pltpu.VMEM)] * 2,
        out_shape=[block, block],
        scratch_shapes=[
            pltpu.VMEM(cotangent.shape, cotangent.dtype),
            pltpu.VMEM(tokens.shape, tokens.dtype),
            pltpu.SemaphoreType.DMA((10,)),
        ],
        cost_estimate=pl.CostEstimate(
            flops=2 * count * features * channels, bytes_accessed=12 << 20, transcendentals=0
        ),
        compiler_params=pltpu.CompilerParams(vmem_limit_bytes=VMEM_GRADIENT),
        name="gradient_blocks",
    )(place, in_hbm(cotangent), in_hbm(tokens))


def frozen_kernel(place, tokens, sibling, here, left, right, far_left, far_right, out, joined):
    depth, count, rows, quarter = here.shape

    @pl.when(pl.program_id(0) == 0)
    def _():
        for shift, ref, first in (
            (0, here, 0), (3, left, 0), (1, right, 0), (2, far_left, 0), (2, far_right, depth // 2)
        ):
            chip = (place[0] + shift) % 4
            lanes = pl.ds(pl.multiple_of((chip % 2) * quarter, quarter), quarter)
            for at in range(ref.shape[0]):
                level = (place[2] + first + at) % 8
                for turn_y in range(count):
                    owner = ((place[1] + turn_y) % 4) * 16 + (chip // 2) * 8 + level
                    span = pl.ds(pl.multiple_of(owner * rows, rows), rows)
                    joined[span, lanes] = ref[at, turn_y]

    for ref, turn_of in ((tokens, pl.program_id(0) < 2), (sibling, pl.program_id(0) >= 2)):

        @pl.when(turn_of)
        def _():
            out[...] = jnp.dot(ref[...], joined[...], preferred_element_type=jnp.float32)


def sigmoid_sums(values):
    rows = values.reshape(LEN // 8, 8, values.shape[1])
    lows = jnp.minimum(rows, 0.0)
    factors = 1.0 + jnp.exp(-jnp.abs(rows))
    low_sum, product = lows[0], factors[0]
    for step in range(1, LEN // 8):
        low_sum = low_sum + lows[step]
        product = product * factors[step]
    return low_sum - jnp.log(product)


def score_kernel(tokens, sibling, halves, frozen, readout, out, joined, held, still, sems):
    quarter = halves.shape[-1]
    count = tokens.shape[0]
    sizes = (LEN,) * 8
    loads, at = [], 0
    for step, size in enumerate(sizes):
        source, first = (tokens, at) if at < count else (sibling, at - count)
        span = pl.ds(at, size)
        loads.append(
            (
                pltpu.make_async_copy(
                    source.at[pl.ds(first, size)], held.at[span], sems.at[2 * step]
                ),
                pltpu.make_async_copy(frozen.at[span], still.at[span], sems.at[2 * step + 1]),
            )
        )
        at += size
    for pair in loads[:AHEAD]:
        for load in pair:
            load.start()
    joined[:, :quarter] = halves[0]
    joined[:, quarter:] = halves[1]
    scale = readout[...]
    lane = lax.broadcasted_iota(jnp.int32, (1, 128), 1)
    parts = jnp.zeros((1, 128), jnp.float32)
    at = 0
    for step, size in enumerate(sizes):
        for load in loads[step]:
            load.wait()
        for load in loads[step + AHEAD] if step + AHEAD < len(sizes) else ():
            load.start()
        values = jnp.dot(held[at : at + size], joined[...], preferred_element_type=jnp.float32)
        blended = blend_rate * values + (1.0 - blend_rate) * still[at : at + size]
        values, blended = values * scale, blended * scale
        for first in range(0, size, LEN):
            rows = slice(first, first + LEN)
            gap = sigmoid_sums(values[rows]) - sigmoid_sums(blended[rows])
            parts = jnp.where(lane == (at + first) // LEN, jnp.sum(gap) / LEN, parts)
        at += size
    out[...] = jnp.broadcast_to(parts[None], out.shape)


def token_specs(count, features):
    rows = count // 2
    return [
        pl.BlockSpec((rows, features), lambda i, *_: (jnp.minimum(i, 1), 0)),
        pl.BlockSpec((rows, features), lambda i, *_: (jnp.maximum(i - 2, 0), 0)),
    ]


def frozen_values(place, tokens, sibling, strips):
    count, features = tokens.shape
    width = 2 * strips[0].shape[-1]
    return pl.pallas_call(
        frozen_kernel,
        grid_spec=pltpu.PrefetchScalarGridSpec(
            num_scalar_prefetch=1,
            grid=(4,),
            in_specs=token_specs(count, features)
            + [pl.BlockSpec(strip.shape, lambda i, *_: (0, 0, 0, 0)) for strip in strips],
            out_specs=pl.BlockSpec((count // 2, width), lambda i, *_: (i, 0)),
            scratch_shapes=[pltpu.VMEM((features, width), jnp.bfloat16)],
        ),
        out_shape=jax.ShapeDtypeStruct((2 * count, width), jnp.float32),
        cost_estimate=pl.CostEstimate(
            flops=4 * count * features * width, bytes_accessed=16 << 20, transcendentals=0
        ),
        compiler_params=pltpu.CompilerParams(vmem_limit_bytes=VMEM),
        name="frozen_values",
    )(place, in_hbm(tokens), in_hbm(sibling), *strips)


def score_sums(tokens, sibling, halves, frozen, readout):
    count, features = tokens.shape
    width = 2 * halves.shape[-1]
    return pl.pallas_call(
        score_kernel,
        out_shape=jax.ShapeDtypeStruct((256, 1, 128), jnp.float32),
        in_specs=[
            pl.BlockSpec(memory_space=pltpu.HBM),
            pl.BlockSpec(memory_space=pltpu.HBM),
            pl.BlockSpec(memory_space=pltpu.VMEM),
            pl.BlockSpec(memory_space=pltpu.HBM),
            pl.BlockSpec(memory_space=pltpu.VMEM),
        ],
        scratch_shapes=[
            pltpu.VMEM((features, width), jnp.bfloat16),
            pltpu.VMEM((2 * count, features), tokens.dtype),
            pltpu.VMEM(frozen.shape, frozen.dtype),
            pltpu.SemaphoreType.DMA((16,)),
        ],
        cost_estimate=pl.CostEstimate(
            flops=4 * count * features * width, bytes_accessed=16 << 20, transcendentals=0
        ),
        compiler_params=pltpu.CompilerParams(vmem_limit_bytes=VMEM_SCORE),
        name="score_sums",
    )(in_hbm(tokens), in_hbm(sibling), halves, in_hbm(frozen), readout)


def plane_sum_kernel(blocks, out):
    total = blocks[0].astype(jnp.float32)
    for at in range(1, blocks.shape[0]):
        total = total + blocks[at].astype(jnp.float32)
    out[...] = total.T.astype(out.dtype)


def plane_sum(blocks):
    _, channels, features = blocks.shape
    return pl.pallas_call(
        plane_sum_kernel,
        out_shape=jax.ShapeDtypeStruct((features, channels), jnp.bfloat16),
        compiler_params=pltpu.CompilerParams(vmem_limit_bytes=16 << 20),
        name="plane_sum",
    )(blocks)


def to_plane(blocks):
    return lax.all_to_all(blocks, PLANE, 0, 0, tiled=True)


def turn(block, shift):
    def index(x):
        return (x % 2) * 2 + x // 2

    return lax.ppermute(
        block, ("xlo", "xhi"), [(index(x), index((x + shift) % 4)) for x in range(4)]
    )


def shift_ring(block, axis, size, shift):
    return lax.ppermute(block, axis, [(i, (i - shift) % size) for i in range(size)])


def gather_z(own):
    own = own[None]
    above, below = shift_ring(own, "z", 8, 1), shift_ring(own, "z", 8, -1)
    upper = shift_ring(jnp.concatenate([below, own, above]), "z", 8, 3)
    lower = shift_ring(jnp.concatenate([own, above]), "z", 8, -3)
    return jnp.concatenate([own, above, upper, lower, below])


def along_z(blocks):
    return lax.all_to_all(blocks, "z", 0, 0, tiled=True)


def shards(tokens, cotangent, policy, anchor, moment, second, readout, pair_index, noisy_flags):
    core = lax.axis_index("core")
    low = lax.axis_index("xlo")
    high = lax.axis_index("xhi")
    rows, channels = policy.shape
    half, quarter = channels // 2, channels // 4
    features = tokens.shape[1]

    def piece(array):
        return lax.dynamic_slice_in_dim(array, (core * 2 + low) * quarter, quarter, axis=1)

    def spread_z(block):
        return along_z(jnp.broadcast_to(block[None], (8, rows, quarter))).reshape(8 * rows, quarter)

    def copies(column):
        return jnp.broadcast_to(column[None], (16,) + column.shape)

    def joined_halves(plane):
        return plane.reshape(2, features, quarter)

    sent, own = gradient_blocks(core[None], cotangent, tokens)
    anchor_piece = piece(anchor).astype(jnp.bfloat16)
    pair = jnp.stack([anchor_piece, shift_ring(anchor_piece, "y", 4, 1)])
    sent, pair = lax.optimization_barrier((sent, pair))
    arrived = lax.ppermute(sent, "core", SWAP)
    strip = jnp.concatenate([pair, shift_ring(pair, "y", 4, 2)])
    blocks = own.astype(jnp.float32) + arrived.astype(jnp.float32)
    blocks, strip = lax.optimization_barrier((blocks.astype(jnp.bfloat16), strip))
    plane = to_plane(blocks.reshape(16, quarter, 8 * rows))
    strips = gather_z(strip)
    plane, strips, tokens = lax.optimization_barrier((plane, strips, tokens))
    sibling = lax.ppermute(tokens, "core", SWAP)
    left, right = turn(strips, 1), turn(strips, -1)
    column = along_z(plane_sum(plane).reshape(8, rows, quarter))
    gradient_piece = jnp.sum(column.astype(jnp.float32), axis=0)

    far_left, far_right = turn(left[:4], 1), turn(right[4:], -1)
    policy_piece = adam_update(
        gradient_piece, piece(policy), piece(anchor), piece(moment), piece(second)
    )[0].astype(jnp.bfloat16)
    other = lax.ppermute(gradient_piece, "xlo", SWAP)
    policy_copies, far_left, far_right, sibling, other = lax.optimization_barrier(
        (copies(spread_z(policy_piece)), far_left, far_right, sibling, other)
    )
    policy_plane = to_plane(policy_copies)
    frozen = frozen_values(
        jnp.stack([high * 2 + low, lax.axis_index("y"), lax.axis_index("z")]), tokens, sibling, (strips, left, right, far_left, far_right)
    )

    strip = jnp.where(
        low == 0,
        jnp.concatenate([gradient_piece, other], axis=1),
        jnp.concatenate([other, gradient_piece], axis=1),
    )
    other = lax.ppermute(strip, "core", SWAP)
    gradient = jnp.where(
        core == 0,
        jnp.concatenate([strip, other], axis=1),
        jnp.concatenate([other, strip], axis=1),
    )
    policy_next, anchor_next, moment_next, second_next = adam_update(
        gradient, policy, anchor, moment, second
    )

    readout_cols = lax.dynamic_slice_in_dim(readout, core * half, half)[None]
    parts = score_sums(tokens, sibling, joined_halves(policy_plane), frozen, readout_cols)
    parts = lax.all_to_all(parts, AXES, 0, 0, tiled=True)
    parts = parts.reshape(2, 2, 64, 128)
    margins = (parts[:, :, :, :4] + parts[:, ::-1, :, 4:8]).reshape(-1)
    pair_loss = pair_losses(margins, pair_index, noisy_flags)
    return (policy_next, anchor_next, moment_next, second_next, pair_loss)


def solution(mesh):
    fine = Mesh(mesh.devices.reshape(2, 2, 4, 2, 8), AXES)
    everywhere = AXES
    owners = ("y", "xhi", "z")
    placed = (
        P(everywhere, None),
        P(everywhere, None),
        P(owners, None),
        P(owners, None),
        P(owners, None),
        P(owners, None),
        P(),
        P(everywhere, None),
        P(everywhere),
    )
    return jax.shard_map(
        shards,
        mesh=fine,
        in_specs=placed,
        out_specs=(
            P(owners, None),
            P(owners, None),
            P(owners, None),
            P(owners, None),
            P(everywhere),
        ),
        check_vma=False,
    )
```

```python
import jax
import jax.numpy as jnp
from jax import lax
from jax.experimental import pallas as pl
from jax.experimental.pallas import tpu as pltpu
from jax.sharding import Mesh
from jax.sharding import PartitionSpec as P

LEN = 192


beta_one = 0.9
beta_two = 0.95
step_count = 20
learn_rate = 0.003
adam_epsilon = 1e-08
blend_rate = 0.6
smoothing = 0.1

AXES = ("xlo", "core", "y", "xhi", "z")
PLANE = ("xlo", "y", "xhi")
SWAP = ((0, 1), (1, 0))


def policy_update(gradient, policy, moment, second):
    moment_new = beta_one * moment + (1.0 - beta_one) * gradient
    second_new = beta_two * second + (1.0 - beta_two) * gradient * gradient
    correct_one = 1.0 - beta_one**step_count
    correct_two = 1.0 - beta_two**step_count
    policy_new = policy - learn_rate * (moment_new / correct_one) / (
        jnp.sqrt(second_new / correct_two) + adam_epsilon
    )
    return (policy_new, moment_new, second_new)


def adam_update(gradient, policy, anchor, moment, second):
    policy_new, moment_new, second_new = policy_update(gradient, policy, moment, second)
    anchor_new = blend_rate * policy_new + (1.0 - blend_rate) * anchor
    return (policy_new, anchor_new, moment_new, second_new)


def pair_losses(margins, pair_index, noisy_flags):
    sequence_index = jnp.arange(margins.shape[0], dtype=jnp.int32)
    chosen = jnp.sum(
        jnp.where(pair_index[:, 0:1] == sequence_index[None, :], margins[None, :], 0.0), axis=1
    )
    rejected = jnp.sum(
        jnp.where(pair_index[:, 1:2] == sequence_index[None, :], margins[None, :], 0.0), axis=1
    )
    margin_gap = chosen - rejected
    logit_value = jnp.where(noisy_flags == 1, -margin_gap, margin_gap)
    return -(1.0 - smoothing) * jax.nn.log_sigmoid(logit_value) - smoothing * jax.nn.log_sigmoid(
        -logit_value
    )


VMEM = 32 << 20
VMEM_GRADIENT = 32 << 20
VMEM_SCORE = 32 << 20
AHEAD = 3


def in_hbm(array):
    return pltpu.with_memory_space_constraint(array, pltpu.HBM)


def gradient_kernel(place, cotangent, tokens, sent, own, held, turned, sems):
    channels = held.shape[1]
    half, quarter = channels // 2, channels // 4
    width = sent.shape[3]
    core = place[0]
    halves = [
        pltpu.make_async_copy(
            cotangent.at[:, pl.ds(pl.multiple_of(which * half, half), half)],
            held.at[:, pl.ds(at * half, half)],
            sems.at[at],
        )
        for at, which in enumerate((1 - core, core))
    ]
    blocks = [
        pltpu.make_async_copy(
            tokens.at[:, pl.ds(at * width, width)],
            turned.at[:, pl.ds(at * width, width)],
            sems.at[2 + at],
        )
        for at in range(8)
    ]
    for load in halves + blocks[:AHEAD]:
        load.start()
    for load in halves:
        load.wait()
    for at, load in enumerate(blocks):
        load.wait()
        if at + AHEAD < len(blocks):
            blocks[at + AHEAD].start()
        product = lax.dot_general(
            held[...],
            turned[:, at * width : (at + 1) * width],
            (((0,), (0,)), ((), ())),
            preferred_element_type=jnp.float32,
        ).astype(sent.dtype)
        sent[0, at] = product[:quarter]
        sent[1, at] = product[quarter:half]
        own[0, at] = product[half : half + quarter]
        own[1, at] = product[half + quarter :]


def gradient_blocks(place, cotangent, tokens):
    count, features = tokens.shape
    channels = cotangent.shape[1]
    quarter = channels // 4
    width = features // 8
    block = pltpu.VMEM((2, 8, quarter, width), jnp.bfloat16)
    return pl.pallas_call(
        gradient_kernel,
        in_specs=[
            pl.BlockSpec(memory_space=pltpu.SMEM),
            pl.BlockSpec(memory_space=pltpu.HBM),
            pl.BlockSpec(memory_space=pltpu.HBM),
        ],
        out_specs=[pl.BlockSpec(memory_space=pltpu.VMEM)] * 2,
        out_shape=[block, block],
        scratch_shapes=[
            pltpu.VMEM(cotangent.shape, cotangent.dtype),
            pltpu.VMEM(tokens.shape, tokens.dtype),
            pltpu.SemaphoreType.DMA((10,)),
        ],
        cost_estimate=pl.CostEstimate(
            flops=2 * count * features * channels, bytes_accessed=12 << 20, transcendentals=0
        ),
        compiler_params=pltpu.CompilerParams(vmem_limit_bytes=VMEM_GRADIENT),
        name="gradient_blocks",
    )(place, in_hbm(cotangent), in_hbm(tokens))


def frozen_kernel(place, tokens, sibling, here, left, right, far_left, far_right, out, joined):
    depth, count, rows, quarter = here.shape

    @pl.when(pl.program_id(0) == 0)
    def _():
        for shift, ref, first in (
            (0, here, 0), (3, left, 0), (1, right, 0), (2, far_left, 0), (2, far_right, depth // 2)
        ):
            chip = (place[0] + shift) % 4
            lanes = pl.ds(pl.multiple_of((chip % 2) * quarter, quarter), quarter)
            for at in range(ref.shape[0]):
                level = (place[2] + first + at) % 8
                for turn_y in range(count):
                    owner = ((place[1] + turn_y) % 4) * 16 + (chip // 2) * 8 + level
                    span = pl.ds(pl.multiple_of(owner * rows, rows), rows)
                    joined[span, lanes] = ref[at, turn_y]

    for ref, turn_of in ((tokens, pl.program_id(0) < 2), (sibling, pl.program_id(0) >= 2)):

        @pl.when(turn_of)
        def _():
            out[...] = jnp.dot(ref[...], joined[...], preferred_element_type=jnp.float32)


def sigmoid_sums(values):
    rows = values.reshape(LEN // 8, 8, values.shape[1])
    lows = jnp.minimum(rows, 0.0)
    factors = 1.0 + jnp.exp(-jnp.abs(rows))
    low_sum, product = lows[0], factors[0]
    for step in range(1, LEN // 8):
        low_sum = low_sum + lows[step]
        product = product * factors[step]
    return low_sum - jnp.log(product)


def score_kernel(tokens, sibling, halves, frozen, readout, out, joined, held, still, sems):
    quarter = halves.shape[-1]
    count = tokens.shape[0]
    sizes = (LEN,) * 8
    loads, at = [], 0
    for step, size in enumerate(sizes):
        source, first = (tokens, at) if at < count else (sibling, at - count)
        span = pl.ds(at, size)
        loads.append(
            (
                pltpu.make_async_copy(
                    source.at[pl.ds(first, size)], held.at[span], sems.at[2 * step]
                ),
                pltpu.make_async_copy(frozen.at[span], still.at[span], sems.at[2 * step + 1]),
            )
        )
        at += size
    for pair in loads[:AHEAD]:
        for load in pair:
            load.start()
    joined[:, :quarter] = halves[0]
    joined[:, quarter:] = halves[1]
    scale = readout[...]
    lane = lax.broadcasted_iota(jnp.int32, (1, 128), 1)
    parts = jnp.zeros((1, 128), jnp.float32)
    at = 0
    for step, size in enumerate(sizes):
        for load in loads[step]:
            load.wait()
        for load in loads[step + AHEAD] if step + AHEAD < len(sizes) else ():
            load.start()
        values = jnp.dot(held[at : at + size], joined[...], preferred_element_type=jnp.float32)
        blended = blend_rate * values + (1.0 - blend_rate) * still[at : at + size]
        values, blended = values * scale, blended * scale
        for first in range(0, size, LEN):
            rows = slice(first, first + LEN)
            gap = sigmoid_sums(values[rows]) - sigmoid_sums(blended[rows])
            parts = jnp.where(lane == (at + first) // LEN, jnp.sum(gap) / LEN, parts)
        at += size
    out[...] = jnp.broadcast_to(parts[None], out.shape)


def token_specs(count, features):
    rows = count // 2
    return [
        pl.BlockSpec((rows, features), lambda i, *_: (jnp.minimum(i, 1), 0)),
        pl.BlockSpec((rows, features), lambda i, *_: (jnp.maximum(i - 2, 0), 0)),
    ]


def frozen_values(place, tokens, sibling, strips):
    count, features = tokens.shape
    width = 2 * strips[0].shape[-1]
    return pl.pallas_call(
        frozen_kernel,
        grid_spec=pltpu.PrefetchScalarGridSpec(
            num_scalar_prefetch=1,
            grid=(4,),
            in_specs=token_specs(count, features)
            + [pl.BlockSpec(strip.shape, lambda i, *_: (0, 0, 0, 0)) for strip in strips],
            out_specs=pl.BlockSpec((count // 2, width), lambda i, *_: (i, 0)),
            scratch_shapes=[pltpu.VMEM((features, width), jnp.bfloat16)],
        ),
        out_shape=jax.ShapeDtypeStruct((2 * count, width), jnp.float32),
        cost_estimate=pl.CostEstimate(
            flops=4 * count * features * width, bytes_accessed=16 << 20, transcendentals=0
        ),
        compiler_params=pltpu.CompilerParams(vmem_limit_bytes=VMEM),
        name="frozen_values",
    )(place, in_hbm(tokens), in_hbm(sibling), *strips)


def score_sums(tokens, sibling, halves, frozen, readout):
    count, features = tokens.shape
    width = 2 * halves.shape[-1]
    return pl.pallas_call(
        score_kernel,
        out_shape=jax.ShapeDtypeStruct((256, 1, 128), jnp.float32),
        in_specs=[
            pl.BlockSpec(memory_space=pltpu.HBM),
            pl.BlockSpec(memory_space=pltpu.HBM),
            pl.BlockSpec(memory_space=pltpu.VMEM),
            pl.BlockSpec(memory_space=pltpu.HBM),
            pl.BlockSpec(memory_space=pltpu.VMEM),
        ],
        scratch_shapes=[
            pltpu.VMEM((features, width), jnp.bfloat16),
            pltpu.VMEM((2 * count, features), tokens.dtype),
            pltpu.VMEM(frozen.shape, frozen.dtype),
            pltpu.SemaphoreType.DMA((16,)),
        ],
        cost_estimate=pl.CostEstimate(
            flops=4 * count * features * width, bytes_accessed=16 << 20, transcendentals=0
        ),
        compiler_params=pltpu.CompilerParams(vmem_limit_bytes=VMEM_SCORE),
        name="score_sums",
    )(in_hbm(tokens), in_hbm(sibling), halves, in_hbm(frozen), readout)


def plane_sum_kernel(blocks, out):
    total = blocks[0].astype(jnp.float32)
    for at in range(1, blocks.shape[0]):
        total = total + blocks[at].astype(jnp.float32)
    out[...] = total.T.astype(out.dtype)


def plane_sum(blocks):
    _, channels, features = blocks.shape
    return pl.pallas_call(
        plane_sum_kernel,
        out_shape=jax.ShapeDtypeStruct((features, channels), jnp.bfloat16),
        compiler_params=pltpu.CompilerParams(vmem_limit_bytes=16 << 20),
        name="plane_sum",
    )(blocks)


def policy_kernel(place, column, policy, moment, second, gradient_out, message):
    quarter = column.shape[2]
    lanes = pl.ds(pl.multiple_of(place[0] * quarter, quarter), quarter)
    gradient = column[0].astype(jnp.float32)
    for at in range(1, column.shape[0]):
        gradient = gradient + column[at].astype(jnp.float32)
    gradient_out[...] = gradient
    updated = policy_update(gradient, policy[:, lanes], moment[:, lanes], second[:, lanes])[0]
    for at in range(message.shape[0]):
        message[at] = updated.astype(message.dtype)


def policy_message(place, column, policy, moment, second):
    return pl.pallas_call(
        policy_kernel,
        in_specs=[pl.BlockSpec(memory_space=pltpu.SMEM)]
        + [pl.BlockSpec(memory_space=pltpu.VMEM)] * 4,
        out_shape=[
            jax.ShapeDtypeStruct(column.shape[1:], jnp.float32),
            jax.ShapeDtypeStruct(column.shape, column.dtype),
        ],
        compiler_params=pltpu.CompilerParams(vmem_limit_bytes=16 << 20),
        name="policy_message",
    )(place, column, policy, moment, second)


def to_plane(blocks):
    return lax.all_to_all(blocks, PLANE, 0, 0, tiled=True)


def turn(block, shift):
    def index(x):
        return (x % 2) * 2 + x // 2

    return lax.ppermute(
        block, ("xlo", "xhi"), [(index(x), index((x + shift) % 4)) for x in range(4)]
    )


def shift_ring(block, axis, size, shift):
    return lax.ppermute(block, axis, [(i, (i - shift) % size) for i in range(size)])


def gather_z(own):
    own = own[None]
    above, below = shift_ring(own, "z", 8, 1), shift_ring(own, "z", 8, -1)
    upper = shift_ring(jnp.concatenate([below, own, above]), "z", 8, 3)
    lower = shift_ring(jnp.concatenate([own, above]), "z", 8, -3)
    return jnp.concatenate([own, above, upper, lower, below])


def along_z(blocks):
    return lax.all_to_all(blocks, "z", 0, 0, tiled=True)


def shards(tokens, cotangent, policy, anchor, moment, second, readout, pair_index, noisy_flags):
    core = lax.axis_index("core")
    low = lax.axis_index("xlo")
    high = lax.axis_index("xhi")
    rows, channels = policy.shape
    half, quarter = channels // 2, channels // 4
    features = tokens.shape[1]

    def piece(array):
        return lax.dynamic_slice_in_dim(array, (core * 2 + low) * quarter, quarter, axis=1)

    def copies(column):
        return jnp.broadcast_to(column[None], (16,) + column.shape)

    def joined_halves(plane):
        return plane.reshape(2, features, quarter)

    sent, own = gradient_blocks(core[None], cotangent, tokens)
    anchor_piece = lax.optimization_barrier(piece(anchor).astype(jnp.bfloat16))
    pair = jnp.stack([anchor_piece, shift_ring(anchor_piece, "y", 4, 1)])
    sent, pair = lax.optimization_barrier((sent, pair))
    arrived = lax.ppermute(sent, "core", SWAP)
    strip = jnp.concatenate([pair, shift_ring(pair, "y", 4, 2)])
    blocks = own.astype(jnp.float32) + arrived.astype(jnp.float32)
    blocks, strip = lax.optimization_barrier((blocks.astype(jnp.bfloat16), strip))
    plane = to_plane(blocks.reshape(16, quarter, 8 * rows))
    strips = gather_z(strip)
    plane, strips, tokens = lax.optimization_barrier((plane, strips, tokens))
    sibling = lax.ppermute(tokens, "core", SWAP)
    left, right = turn(strips, 1), turn(strips, -1)
    column = along_z(plane_sum(plane).reshape(8, rows, quarter))
    far_left, far_right = turn(left[:4], 1), turn(right[4:], -1)
    gradient_piece, message = policy_message(
        (core * 2 + low)[None], column, policy, moment, second
    )
    policy_column = along_z(message).reshape(8 * rows, quarter)
    other = lax.ppermute(gradient_piece, "xlo", SWAP)
    policy_copies, far_left, far_right, sibling, other = lax.optimization_barrier(
        (copies(policy_column), far_left, far_right, sibling, other)
    )
    policy_plane = to_plane(policy_copies)
    frozen = frozen_values(
        jnp.stack([high * 2 + low, lax.axis_index("y"), lax.axis_index("z")]), tokens, sibling, (strips, left, right, far_left, far_right)
    )

    strip = jnp.where(
        low == 0,
        jnp.concatenate([gradient_piece, other], axis=1),
        jnp.concatenate([other, gradient_piece], axis=1),
    )
    other = lax.ppermute(strip, "core", SWAP)
    gradient = jnp.where(
        core == 0,
        jnp.concatenate([strip, other], axis=1),
        jnp.concatenate([other, strip], axis=1),
    )
    policy_next, anchor_next, moment_next, second_next = adam_update(
        gradient, policy, anchor, moment, second
    )

    readout_cols = lax.dynamic_slice_in_dim(readout, core * half, half)[None]
    parts = score_sums(tokens, sibling, joined_halves(policy_plane), frozen, readout_cols)
    parts = lax.all_to_all(parts, AXES, 0, 0, tiled=True)
    parts = parts.reshape(2, 2, 64, 128)
    margins = (parts[:, :, :, :4] + parts[:, ::-1, :, 4:8]).reshape(-1)
    pair_loss = pair_losses(margins, pair_index, noisy_flags)
    return (policy_next, anchor_next, moment_next, second_next, pair_loss)


def solution(mesh):
    fine = Mesh(mesh.devices.reshape(2, 2, 4, 2, 8), AXES)
    everywhere = AXES
    owners = ("y", "xhi", "z")
    placed = (
        P(everywhere, None),
        P(everywhere, None),
        P(owners, None),
        P(owners, None),
        P(owners, None),
        P(owners, None),
        P(),
        P(everywhere, None),
        P(everywhere),
    )
    return jax.shard_map(
        shards,
        mesh=fine,
        in_specs=placed,
        out_specs=(
            P(owners, None),
            P(owners, None),
            P(owners, None),
            P(owners, None),
            P(everywhere),
        ),
        check_vma=False,
    )
```

```python
import jax
import jax.numpy as jnp
from jax import lax
from jax.experimental import pallas as pl
from jax.experimental.pallas import tpu as pltpu
from jax.sharding import Mesh
from jax.sharding import PartitionSpec as P

LEN = 192


beta_one = 0.9
beta_two = 0.95
step_count = 20
learn_rate = 0.003
adam_epsilon = 1e-08
blend_rate = 0.6
smoothing = 0.1

AXES = ("xlo", "core", "y", "xhi", "z")
PLANE = ("xlo", "y", "xhi")
SWAP = ((0, 1), (1, 0))


def policy_update(gradient, policy, moment, second):
    moment_new = beta_one * moment + (1.0 - beta_one) * gradient
    second_new = beta_two * second + (1.0 - beta_two) * gradient * gradient
    correct_one = 1.0 - beta_one**step_count
    correct_two = 1.0 - beta_two**step_count
    policy_new = policy - learn_rate * (moment_new / correct_one) / (
        jnp.sqrt(second_new / correct_two) + adam_epsilon
    )
    return (policy_new, moment_new, second_new)


def adam_update(gradient, policy, anchor, moment, second):
    policy_new, moment_new, second_new = policy_update(gradient, policy, moment, second)
    anchor_new = blend_rate * policy_new + (1.0 - blend_rate) * anchor
    return (policy_new, anchor_new, moment_new, second_new)


def pair_losses(margins, pair_index, noisy_flags):
    sequence_index = jnp.arange(margins.shape[0], dtype=jnp.int32)
    chosen = jnp.sum(
        jnp.where(pair_index[:, 0:1] == sequence_index[None, :], margins[None, :], 0.0), axis=1
    )
    rejected = jnp.sum(
        jnp.where(pair_index[:, 1:2] == sequence_index[None, :], margins[None, :], 0.0), axis=1
    )
    margin_gap = chosen - rejected
    logit_value = jnp.where(noisy_flags == 1, -margin_gap, margin_gap)
    return -(1.0 - smoothing) * jax.nn.log_sigmoid(logit_value) - smoothing * jax.nn.log_sigmoid(
        -logit_value
    )


VMEM = 32 << 20
VMEM_GRADIENT = 32 << 20
AHEAD = 3


def in_hbm(array):
    return pltpu.with_memory_space_constraint(array, pltpu.HBM)


def gradient_kernel(place, cotangent, tokens, sent, own, held, turned, sems):
    channels = held.shape[1]
    half, quarter = channels // 2, channels // 4
    width = sent.shape[3]
    core = place[0]
    halves = [
        pltpu.make_async_copy(
            cotangent.at[:, pl.ds(pl.multiple_of(which * half, half), half)],
            held.at[:, pl.ds(at * half, half)],
            sems.at[at],
        )
        for at, which in enumerate((1 - core, core))
    ]
    blocks = [
        pltpu.make_async_copy(
            tokens.at[:, pl.ds(at * width, width)],
            turned.at[:, pl.ds(at * width, width)],
            sems.at[2 + at],
        )
        for at in range(8)
    ]
    for load in halves + blocks[:AHEAD]:
        load.start()
    for load in halves:
        load.wait()
    for at, load in enumerate(blocks):
        load.wait()
        if at + AHEAD < len(blocks):
            blocks[at + AHEAD].start()
        product = lax.dot_general(
            held[...],
            turned[:, at * width : (at + 1) * width],
            (((0,), (0,)), ((), ())),
            preferred_element_type=jnp.float32,
        ).astype(sent.dtype)
        sent[0, at] = product[:quarter]
        sent[1, at] = product[quarter:half]
        own[0, at] = product[half : half + quarter]
        own[1, at] = product[half + quarter :]


def gradient_blocks(place, cotangent, tokens):
    count, features = tokens.shape
    channels = cotangent.shape[1]
    quarter = channels // 4
    width = features // 8
    block = pltpu.VMEM((2, 8, quarter, width), jnp.bfloat16)
    return pl.pallas_call(
        gradient_kernel,
        in_specs=[
            pl.BlockSpec(memory_space=pltpu.SMEM),
            pl.BlockSpec(memory_space=pltpu.HBM),
            pl.BlockSpec(memory_space=pltpu.HBM),
        ],
        out_specs=[pl.BlockSpec(memory_space=pltpu.VMEM)] * 2,
        out_shape=[block, block],
        scratch_shapes=[
            pltpu.VMEM(cotangent.shape, cotangent.dtype),
            pltpu.VMEM(tokens.shape, tokens.dtype),
            pltpu.SemaphoreType.DMA((10,)),
        ],
        cost_estimate=pl.CostEstimate(
            flops=2 * count * features * channels, bytes_accessed=12 << 20, transcendentals=0
        ),
        compiler_params=pltpu.CompilerParams(vmem_limit_bytes=VMEM_GRADIENT),
        name="gradient_blocks",
    )(place, in_hbm(cotangent), in_hbm(tokens))


def chunk_loads(source, target, sems):
    return [
        pltpu.make_async_copy(
            source.at[pl.ds(at * LEN, LEN)], target.at[pl.ds(at * LEN, LEN)], sems.at[at]
        )
        for at in range(source.shape[0] // LEN)
    ]


def product_kernel(tokens, own, sibling, out, out_sibling, held, sems):
    loads = chunk_loads(tokens, held, sems)
    for load in loads:
        load.start()
    for at, load in enumerate(loads):
        load.wait()
        span = slice(at * LEN, (at + 1) * LEN)
        for weights, target in ((own, out), (sibling, out_sibling)):
            target[span] = jnp.dot(held[span], weights[...], preferred_element_type=jnp.float32)


def assemble_kernel(place, here, left, right, far_left, far_right, joined):
    depth, count, rows, quarter = here.shape
    for shift, ref, first in (
        (0, here, 0), (3, left, 0), (1, right, 0), (2, far_left, 0), (2, far_right, depth // 2)
    ):
        chip = (place[0] + shift) % 4
        lanes = pl.ds(pl.multiple_of((chip % 2) * quarter, quarter), quarter)
        for at in range(ref.shape[0]):
            level = (place[2] + first + at) % 8
            for turn_y in range(count):
                owner = ((place[1] + turn_y) % 4) * 16 + (chip // 2) * 8 + level
                span = pl.ds(pl.multiple_of(owner * rows, rows), rows)
                joined[span, lanes] = ref[at, turn_y]


def sigmoid_sums(values):
    rows = values.reshape(LEN // 8, 8, values.shape[1])
    lows = jnp.minimum(rows, 0.0)
    factors = 1.0 + jnp.exp(-jnp.abs(rows))
    low_sum, product = lows[0], factors[0]
    for step in range(1, LEN // 8):
        low_sum = low_sum + lows[step]
        product = product * factors[step]
    return low_sum - jnp.log(product)


def chunk_scores(tokens, weights, frozen, scale, at):
    span = slice(at * LEN, (at + 1) * LEN)
    values = jnp.dot(tokens[span], weights[...], preferred_element_type=jnp.float32)
    blended = blend_rate * values + (1.0 - blend_rate) * frozen[span]
    gap = sigmoid_sums(values * scale) - sigmoid_sums(blended * scale)
    lane = lax.broadcasted_iota(jnp.int32, (1, 128), 1)
    return jnp.where(lane == at, jnp.sum(gap) / LEN, 0.0)


def join(halves, joined):
    quarter = halves.shape[-1]
    joined[:, :quarter] = halves[0]
    joined[:, quarter:] = halves[1]


def own_kernel(tokens, halves, frozen, readout, parts, kept, joined, still, sems, still_sems):
    loads = chunk_loads(tokens, kept, sems)
    still_loads = chunk_loads(frozen, still, still_sems)
    for pair in zip(loads, still_loads):
        for load in pair:
            load.start()
    join(halves, joined)
    scale = readout[...]
    total = jnp.zeros((1, 128), jnp.float32)
    for at in range(len(loads)):
        loads[at].wait()
        still_loads[at].wait()
        total = total + chunk_scores(kept, joined, still, scale, at)
    parts[...] = total


def sibling_kernel(tokens, halves, frozen, readout, parts, out, joined, still, sems):
    loads = chunk_loads(frozen, still, sems)
    for load in loads:
        load.start()
    join(halves, joined)
    scale = readout[...]
    total = parts[...]
    for at in range(len(loads)):
        loads[at].wait()
        total = total + chunk_scores(tokens, joined, still, scale, at)
    out[...] = jnp.broadcast_to(total[None], out.shape)


def in_vmem(number):
    return [pl.BlockSpec(memory_space=pltpu.VMEM)] * number


def work(tokens, width, kept):
    count, features = tokens.shape
    return pl.CostEstimate(
        flops=2 * count * features * width, bytes_accessed=kept << 20, transcendentals=0
    )


def anchor_columns(place, features, strips):
    return pl.pallas_call(
        assemble_kernel,
        in_specs=[pl.BlockSpec(memory_space=pltpu.SMEM)] + in_vmem(5),
        out_shape=jax.ShapeDtypeStruct((features, 2 * strips[0].shape[-1]), jnp.bfloat16),
        compiler_params=pltpu.CompilerParams(vmem_limit_bytes=16 << 20),
        name="anchor_columns",
    )(place, *strips)


def frozen_values(tokens, own, sibling):
    count, width = tokens.shape[0], own.shape[1]
    out = jax.ShapeDtypeStruct((count, width), jnp.float32)
    return pl.pallas_call(
        product_kernel,
        in_specs=[pl.BlockSpec(memory_space=pltpu.HBM)] + in_vmem(2),
        out_shape=[out, out],
        scratch_shapes=[
            pltpu.VMEM(tokens.shape, tokens.dtype),
            pltpu.SemaphoreType.DMA((count // LEN,)),
        ],
        cost_estimate=work(tokens, 2 * width, 12),
        compiler_params=pltpu.CompilerParams(vmem_limit_bytes=VMEM),
        name="frozen_values",
    )(in_hbm(tokens), own, sibling)


def own_scores(tokens, halves, frozen, readout):
    count, features = tokens.shape
    width = 2 * halves.shape[-1]
    return pl.pallas_call(
        own_kernel,
        in_specs=[
            pl.BlockSpec(memory_space=pltpu.HBM),
            pl.BlockSpec(memory_space=pltpu.VMEM),
            pl.BlockSpec(memory_space=pltpu.HBM),
            pl.BlockSpec(memory_space=pltpu.VMEM),
        ],
        out_specs=in_vmem(2),
        out_shape=[
            jax.ShapeDtypeStruct((1, 128), jnp.float32),
            pltpu.VMEM(tokens.shape, tokens.dtype),
        ],
        scratch_shapes=[
            pltpu.VMEM((features, width), jnp.bfloat16),
            pltpu.VMEM(frozen.shape, frozen.dtype),
            pltpu.SemaphoreType.DMA((count // LEN,)),
            pltpu.SemaphoreType.DMA((count // LEN,)),
        ],
        cost_estimate=work(tokens, width, 9),
        compiler_params=pltpu.CompilerParams(vmem_limit_bytes=VMEM),
        name="own_scores",
    )(in_hbm(tokens), halves, in_hbm(frozen), readout)


def sibling_scores(tokens, halves, frozen, readout, parts):
    count, features = tokens.shape
    width = 2 * halves.shape[-1]
    return pl.pallas_call(
        sibling_kernel,
        in_specs=in_vmem(2) + [pl.BlockSpec(memory_space=pltpu.HBM)] + in_vmem(2),
        out_shape=jax.ShapeDtypeStruct((256, 1, 128), jnp.float32),
        scratch_shapes=[
            pltpu.VMEM((features, width), jnp.bfloat16),
            pltpu.VMEM(frozen.shape, frozen.dtype),
            pltpu.SemaphoreType.DMA((count // LEN,)),
        ],
        cost_estimate=work(tokens, width, 3),
        compiler_params=pltpu.CompilerParams(vmem_limit_bytes=VMEM),
        name="sibling_scores",
    )(
        pltpu.with_memory_space_constraint(tokens, pltpu.VMEM),
        halves,
        in_hbm(frozen),
        readout,
        parts,
    )


def plane_sum_kernel(blocks, out):
    total = blocks[0].astype(jnp.float32)
    for at in range(1, blocks.shape[0]):
        total = total + blocks[at].astype(jnp.float32)
    out[...] = total.T.astype(out.dtype)


def plane_sum(blocks):
    _, channels, features = blocks.shape
    return pl.pallas_call(
        plane_sum_kernel,
        out_shape=jax.ShapeDtypeStruct((features, channels), jnp.bfloat16),
        compiler_params=pltpu.CompilerParams(vmem_limit_bytes=16 << 20),
        name="plane_sum",
    )(blocks)


def policy_kernel(place, column, policy, moment, second, gradient_out, message):
    quarter = column.shape[2]
    lanes = pl.ds(pl.multiple_of(place[0] * quarter, quarter), quarter)
    gradient = column[0].astype(jnp.float32)
    for at in range(1, column.shape[0]):
        gradient = gradient + column[at].astype(jnp.float32)
    gradient_out[...] = gradient
    updated = policy_update(gradient, policy[:, lanes], moment[:, lanes], second[:, lanes])[0]
    for at in range(message.shape[0]):
        message[at] = updated.astype(message.dtype)


def policy_message(place, column, policy, moment, second):
    return pl.pallas_call(
        policy_kernel,
        in_specs=[pl.BlockSpec(memory_space=pltpu.SMEM)]
        + [pl.BlockSpec(memory_space=pltpu.VMEM)] * 4,
        out_shape=[
            jax.ShapeDtypeStruct(column.shape[1:], jnp.float32),
            jax.ShapeDtypeStruct(column.shape, column.dtype),
        ],
        compiler_params=pltpu.CompilerParams(vmem_limit_bytes=16 << 20),
        name="policy_message",
    )(place, column, policy, moment, second)


def to_plane(blocks):
    return lax.all_to_all(blocks, PLANE, 0, 0, tiled=True)


def turn(block, shift):
    def index(x):
        return (x % 2) * 2 + x // 2

    return lax.ppermute(
        block, ("xlo", "xhi"), [(index(x), index((x + shift) % 4)) for x in range(4)]
    )


def shift_ring(block, axis, size, shift):
    return lax.ppermute(block, axis, [(i, (i - shift) % size) for i in range(size)])


def gather_z(own):
    own = own[None]
    above, below = shift_ring(own, "z", 8, 1), shift_ring(own, "z", 8, -1)
    upper = shift_ring(jnp.concatenate([below, own, above]), "z", 8, 3)
    lower = shift_ring(jnp.concatenate([own, above]), "z", 8, -3)
    return jnp.concatenate([own, above, upper, lower, below])


def along_z(blocks):
    return lax.all_to_all(blocks, "z", 0, 0, tiled=True)


def shards(tokens, cotangent, policy, anchor, moment, second, readout, pair_index, noisy_flags):
    core = lax.axis_index("core")
    low = lax.axis_index("xlo")
    high = lax.axis_index("xhi")
    rows, channels = policy.shape
    half, quarter = channels // 2, channels // 4
    features = tokens.shape[1]

    def piece(array):
        return lax.dynamic_slice_in_dim(array, (core * 2 + low) * quarter, quarter, axis=1)

    def copies(column):
        return jnp.broadcast_to(column[None], (16,) + column.shape)

    def joined_halves(plane):
        return plane.reshape(2, features, quarter)

    sent, own = gradient_blocks(core[None], cotangent, tokens)
    anchor_piece = lax.optimization_barrier(piece(anchor).astype(jnp.bfloat16))
    pair = jnp.stack([anchor_piece, shift_ring(anchor_piece, "y", 4, 1)])
    sent, pair = lax.optimization_barrier((sent, pair))
    arrived = lax.ppermute(sent, "core", SWAP)
    strip = jnp.concatenate([pair, shift_ring(pair, "y", 4, 2)])
    blocks = own.astype(jnp.float32) + arrived.astype(jnp.float32)
    blocks, strip = lax.optimization_barrier((blocks.astype(jnp.bfloat16), strip))
    plane = to_plane(blocks.reshape(16, quarter, 8 * rows))
    strips = gather_z(strip)
    plane, strips = lax.optimization_barrier((plane, strips))
    left, right = turn(strips, 1), turn(strips, -1)
    column = along_z(plane_sum(plane).reshape(8, rows, quarter))
    far_left, far_right = turn(left[:4], 1), turn(right[4:], -1)
    gradient_piece, message = policy_message(
        (core * 2 + low)[None], column, policy, moment, second
    )
    policy_column = along_z(message).reshape(8 * rows, quarter)
    other = lax.ppermute(gradient_piece, "xlo", SWAP)
    policy_copies, far_left, far_right, other = lax.optimization_barrier(
        (copies(policy_column), far_left, far_right, other)
    )
    policy_plane = to_plane(policy_copies)
    anchor_half = anchor_columns(
        jnp.stack([high * 2 + low, lax.axis_index("y"), lax.axis_index("z")]),
        features,
        (strips, left, right, far_left, far_right),
    )
    frozen, frozen_sibling = frozen_values(
        tokens, anchor_half, lax.ppermute(anchor_half, "core", SWAP)
    )

    strip = jnp.where(
        low == 0,
        jnp.concatenate([gradient_piece, other], axis=1),
        jnp.concatenate([other, gradient_piece], axis=1),
    )
    other = lax.ppermute(strip, "core", SWAP)
    gradient = jnp.where(
        core == 0,
        jnp.concatenate([strip, other], axis=1),
        jnp.concatenate([other, strip], axis=1),
    )
    policy_next, anchor_next, moment_next, second_next = adam_update(
        gradient, policy, anchor, moment, second
    )

    def readout_half(which):
        return lax.dynamic_slice_in_dim(readout, which * half, half)[None]

    policy_plane, frozen, frozen_sibling = lax.optimization_barrier(
        (policy_plane, frozen, frozen_sibling)
    )
    halves = joined_halves(policy_plane)
    halves_sibling = lax.ppermute(halves, "core", SWAP)
    parts, kept = own_scores(tokens, halves, frozen, readout_half(core))
    parts = sibling_scores(kept, halves_sibling, frozen_sibling, readout_half(1 - core), parts)
    margins = lax.all_to_all(parts, AXES, 0, 0, tiled=True)[:, 0, :4].reshape(-1)
    pair_loss = pair_losses(margins, pair_index, noisy_flags)
    return (policy_next, anchor_next, moment_next, second_next, pair_loss)


def solution(mesh):
    fine = Mesh(mesh.devices.reshape(2, 2, 4, 2, 8), AXES)
    everywhere = AXES
    owners = ("y", "xhi", "z")
    placed = (
        P(everywhere, None),
        P(everywhere, None),
        P(owners, None),
        P(owners, None),
        P(owners, None),
        P(owners, None),
        P(),
        P(everywhere, None),
        P(everywhere),
    )
    return jax.shard_map(
        shards,
        mesh=fine,
        in_specs=placed,
        out_specs=(
            P(owners, None),
            P(owners, None),
            P(owners, None),
            P(owners, None),
            P(everywhere),
        ),
        check_vma=False,
    )
```

```python
import jax
import jax.numpy as jnp
from jax import lax
from jax.experimental import pallas as pl
from jax.experimental.pallas import tpu as pltpu
from jax.sharding import Mesh
from jax.sharding import PartitionSpec as P

LEN = 192


beta_one = 0.9
beta_two = 0.95
step_count = 20
learn_rate = 0.003
adam_epsilon = 1e-08
blend_rate = 0.6
smoothing = 0.1

AXES = ("xlo", "core", "y", "xhi", "z")
PLANE = ("xlo", "y", "xhi")
SWAP = ((0, 1), (1, 0))


def policy_update(gradient, policy, moment, second):
    moment_new = beta_one * moment + (1.0 - beta_one) * gradient
    second_new = beta_two * second + (1.0 - beta_two) * gradient * gradient
    correct_one = 1.0 - beta_one**step_count
    correct_two = 1.0 - beta_two**step_count
    policy_new = policy - learn_rate * (moment_new / correct_one) / (
        jnp.sqrt(second_new / correct_two) + adam_epsilon
    )
    return (policy_new, moment_new, second_new)


def adam_update(gradient, policy, anchor, moment, second):
    policy_new, moment_new, second_new = policy_update(gradient, policy, moment, second)
    anchor_new = blend_rate * policy_new + (1.0 - blend_rate) * anchor
    return (policy_new, anchor_new, moment_new, second_new)


def pair_losses(margins, pair_index, noisy_flags):
    sequence_index = jnp.arange(margins.shape[0], dtype=jnp.int32)
    chosen = jnp.sum(
        jnp.where(pair_index[:, 0:1] == sequence_index[None, :], margins[None, :], 0.0), axis=1
    )
    rejected = jnp.sum(
        jnp.where(pair_index[:, 1:2] == sequence_index[None, :], margins[None, :], 0.0), axis=1
    )
    margin_gap = chosen - rejected
    logit_value = jnp.where(noisy_flags == 1, -margin_gap, margin_gap)
    return -(1.0 - smoothing) * jax.nn.log_sigmoid(logit_value) - smoothing * jax.nn.log_sigmoid(
        -logit_value
    )


VMEM = 32 << 20
VMEM_GRADIENT = 32 << 20
VMEM_SCORE = 32 << 20
AHEAD = 3


def in_hbm(array):
    return pltpu.with_memory_space_constraint(array, pltpu.HBM)


def gradient_kernel(place, cotangent, tokens, sent, own, held, turned, sems):
    channels = held.shape[1]
    half, quarter = channels // 2, channels // 4
    width = sent.shape[3]
    core = place[0]
    halves = [
        pltpu.make_async_copy(
            cotangent.at[:, pl.ds(pl.multiple_of(which * half, half), half)],
            held.at[:, pl.ds(at * half, half)],
            sems.at[at],
        )
        for at, which in enumerate((1 - core, core))
    ]
    blocks = [
        pltpu.make_async_copy(
            tokens.at[:, pl.ds(at * width, width)],
            turned.at[:, pl.ds(at * width, width)],
            sems.at[2 + at],
        )
        for at in range(8)
    ]
    for load in halves + blocks[:AHEAD]:
        load.start()
    for load in halves:
        load.wait()
    for at, load in enumerate(blocks):
        load.wait()
        if at + AHEAD < len(blocks):
            blocks[at + AHEAD].start()
        product = lax.dot_general(
            held[...],
            turned[:, at * width : (at + 1) * width],
            (((0,), (0,)), ((), ())),
            preferred_element_type=jnp.float32,
        ).astype(sent.dtype)
        sent[0, at] = product[:quarter]
        sent[1, at] = product[quarter:half]
        own[0, at] = product[half : half + quarter]
        own[1, at] = product[half + quarter :]


def gradient_blocks(place, cotangent, tokens):
    count, features = tokens.shape
    channels = cotangent.shape[1]
    quarter = channels // 4
    width = features // 8
    block = pltpu.VMEM((2, 8, quarter, width), jnp.bfloat16)
    return pl.pallas_call(
        gradient_kernel,
        in_specs=[
            pl.BlockSpec(memory_space=pltpu.SMEM),
            pl.BlockSpec(memory_space=pltpu.HBM),
            pl.BlockSpec(memory_space=pltpu.HBM),
        ],
        out_specs=[pl.BlockSpec(memory_space=pltpu.VMEM)] * 2,
        out_shape=[block, block],
        scratch_shapes=[
            pltpu.VMEM(cotangent.shape, cotangent.dtype),
            pltpu.VMEM(tokens.shape, tokens.dtype),
            pltpu.SemaphoreType.DMA((10,)),
        ],
        cost_estimate=pl.CostEstimate(
            flops=2 * count * features * channels, bytes_accessed=12 << 20, transcendentals=0
        ),
        compiler_params=pltpu.CompilerParams(vmem_limit_bytes=VMEM_GRADIENT),
        name="gradient_blocks",
    )(place, in_hbm(cotangent), in_hbm(tokens))


def frozen_kernel(place, tokens, sibling, here, left, right, far_left, far_right, out, joined):
    depth, count, rows, quarter = here.shape

    @pl.when(pl.program_id(0) == 0)
    def _():
        for shift, ref, first in (
            (0, here, 0), (3, left, 0), (1, right, 0), (2, far_left, 0), (2, far_right, depth // 2)
        ):
            chip = (place[0] + shift) % 4
            lanes = pl.ds(pl.multiple_of((chip % 2) * quarter, quarter), quarter)
            for at in range(ref.shape[0]):
                level = (place[2] + first + at) % 8
                for turn_y in range(count):
                    owner = ((place[1] + turn_y) % 4) * 16 + (chip // 2) * 8 + level
                    span = pl.ds(pl.multiple_of(owner * rows, rows), rows)
                    joined[span, lanes] = ref[at, turn_y]

    for ref, turn_of in ((tokens, pl.program_id(0) < 2), (sibling, pl.program_id(0) >= 2)):

        @pl.when(turn_of)
        def _():
            out[...] = jnp.dot(ref[...], joined[...], preferred_element_type=jnp.float32)


def sigmoid_sums(values):
    rows = values.reshape(LEN // 8, 8, values.shape[1])
    lows = jnp.minimum(rows, 0.0)
    factors = 1.0 + jnp.exp(-jnp.abs(rows))
    low_sum, product = lows[0], factors[0]
    for step in range(1, LEN // 8):
        low_sum = low_sum + lows[step]
        product = product * factors[step]
    return low_sum - jnp.log(product)


def score_kernel(tokens, sibling, halves, frozen, readout, out, joined, held, still, sems):
    quarter = halves.shape[-1]
    count = tokens.shape[0]
    sizes = (2 * LEN,) * 4
    loads, at = [], 0
    for step, size in enumerate(sizes):
        source, first = (tokens, at) if at < count else (sibling, at - count)
        span = pl.ds(at, size)
        loads.append(
            (
                pltpu.make_async_copy(
                    source.at[pl.ds(first, size)], held.at[span], sems.at[2 * step]
                ),
                pltpu.make_async_copy(frozen.at[span], still.at[span], sems.at[2 * step + 1]),
            )
        )
        at += size
    for pair in loads[:2]:
        for load in pair:
            load.start()
    joined[:, :quarter] = halves[0]
    joined[:, quarter:] = halves[1]
    scale = readout[...]
    lane = lax.broadcasted_iota(jnp.int32, (1, 128), 1)
    parts = jnp.zeros((1, 128), jnp.float32)
    at = 0
    for step, size in enumerate(sizes):
        for load in loads[step]:
            load.wait()
        for load in loads[step + 2] if step + 2 < len(sizes) else ():
            load.start()
        values = jnp.dot(held[at : at + size], joined[...], preferred_element_type=jnp.float32)
        blended = blend_rate * values + (1.0 - blend_rate) * still[at : at + size]
        values, blended = values * scale, blended * scale
        for first in range(0, size, LEN):
            rows = slice(first, first + LEN)
            gap = sigmoid_sums(values[rows]) - sigmoid_sums(blended[rows])
            parts = jnp.where(lane == (at + first) // LEN, jnp.sum(gap) / LEN, parts)
        at += size
    out[...] = jnp.broadcast_to(parts[None], out.shape)


def token_specs(count, features):
    rows = count // 2
    return [
        pl.BlockSpec((rows, features), lambda i, *_: (jnp.minimum(i, 1), 0)),
        pl.BlockSpec((rows, features), lambda i, *_: (jnp.maximum(i - 2, 0), 0)),
    ]


def frozen_values(place, tokens, sibling, strips):
    count, features = tokens.shape
    width = 2 * strips[0].shape[-1]
    return pl.pallas_call(
        frozen_kernel,
        grid_spec=pltpu.PrefetchScalarGridSpec(
            num_scalar_prefetch=1,
            grid=(4,),
            in_specs=token_specs(count, features)
            + [pl.BlockSpec(strip.shape, lambda i, *_: (0, 0, 0, 0)) for strip in strips],
            out_specs=pl.BlockSpec((count // 2, width), lambda i, *_: (i, 0)),
            scratch_shapes=[pltpu.VMEM((features, width), jnp.bfloat16)],
        ),
        out_shape=jax.ShapeDtypeStruct((2 * count, width), jnp.float32),
        cost_estimate=pl.CostEstimate(
            flops=4 * count * features * width, bytes_accessed=16 << 20, transcendentals=0
        ),
        compiler_params=pltpu.CompilerParams(vmem_limit_bytes=VMEM),
        name="frozen_values",
    )(place, in_hbm(tokens), in_hbm(sibling), *strips)


def score_sums(tokens, sibling, halves, frozen, readout):
    count, features = tokens.shape
    width = 2 * halves.shape[-1]
    return pl.pallas_call(
        score_kernel,
        out_shape=jax.ShapeDtypeStruct((256, 1, 128), jnp.float32),
        in_specs=[
            pl.BlockSpec(memory_space=pltpu.HBM),
            pl.BlockSpec(memory_space=pltpu.HBM),
            pl.BlockSpec(memory_space=pltpu.VMEM),
            pl.BlockSpec(memory_space=pltpu.HBM),
            pl.BlockSpec(memory_space=pltpu.VMEM),
        ],
        scratch_shapes=[
            pltpu.VMEM((features, width), jnp.bfloat16),
            pltpu.VMEM((2 * count, features), tokens.dtype),
            pltpu.VMEM(frozen.shape, frozen.dtype),
            pltpu.SemaphoreType.DMA((8,)),
        ],
        cost_estimate=pl.CostEstimate(
            flops=4 * count * features * width, bytes_accessed=16 << 20, transcendentals=0
        ),
        compiler_params=pltpu.CompilerParams(vmem_limit_bytes=VMEM_SCORE),
        name="score_sums",
    )(in_hbm(tokens), in_hbm(sibling), halves, in_hbm(frozen), readout)


def plane_sum_kernel(blocks, out):
    total = blocks[0].astype(jnp.float32)
    for at in range(1, blocks.shape[0]):
        total = total + blocks[at].astype(jnp.float32)
    out[...] = total.T.astype(out.dtype)


def plane_sum(blocks):
    _, channels, features = blocks.shape
    return pl.pallas_call(
        plane_sum_kernel,
        out_shape=jax.ShapeDtypeStruct((features, channels), jnp.bfloat16),
        compiler_params=pltpu.CompilerParams(vmem_limit_bytes=16 << 20),
        name="plane_sum",
    )(blocks)


def policy_kernel(place, column, policy, moment, second, gradient_out, message):
    quarter = column.shape[2]
    lanes = pl.ds(pl.multiple_of(place[0] * quarter, quarter), quarter)
    gradient = column[0].astype(jnp.float32)
    for at in range(1, column.shape[0]):
        gradient = gradient + column[at].astype(jnp.float32)
    gradient_out[...] = gradient
    updated = policy_update(gradient, policy[:, lanes], moment[:, lanes], second[:, lanes])[0]
    for at in range(message.shape[0]):
        message[at] = updated.astype(message.dtype)


def policy_message(place, column, policy, moment, second):
    return pl.pallas_call(
        policy_kernel,
        in_specs=[pl.BlockSpec(memory_space=pltpu.SMEM)]
        + [pl.BlockSpec(memory_space=pltpu.VMEM)] * 4,
        out_shape=[
            jax.ShapeDtypeStruct(column.shape[1:], jnp.float32),
            jax.ShapeDtypeStruct(column.shape, column.dtype),
        ],
        compiler_params=pltpu.CompilerParams(vmem_limit_bytes=16 << 20),
        name="policy_message",
    )(place, column, policy, moment, second)


def copies_kernel(column, out, sems):
    sends = [pltpu.make_async_copy(column, out.at[at], sems.at[at]) for at in range(out.shape[0])]
    for send in sends:
        send.start()
    for send in sends:
        send.wait()


def plane_copies(column):
    return pl.pallas_call(
        copies_kernel,
        in_specs=[pl.BlockSpec(memory_space=pltpu.VMEM)],
        out_specs=pl.BlockSpec(memory_space=pltpu.HBM),
        out_shape=jax.ShapeDtypeStruct((16,) + column.shape, column.dtype),
        scratch_shapes=[pltpu.SemaphoreType.DMA((16,))],
        compiler_params=pltpu.CompilerParams(vmem_limit_bytes=16 << 20),
        name="plane_copies",
    )(column)


def to_plane(blocks):
    return lax.all_to_all(blocks, PLANE, 0, 0, tiled=True)


def turn(block, shift):
    def index(x):
        return (x % 2) * 2 + x // 2

    return lax.ppermute(
        block, ("xlo", "xhi"), [(index(x), index((x + shift) % 4)) for x in range(4)]
    )


def shift_ring(block, axis, size, shift):
    return lax.ppermute(block, axis, [(i, (i - shift) % size) for i in range(size)])


def gather_z(own):
    own = own[None]
    above, below = shift_ring(own, "z", 8, 1), shift_ring(own, "z", 8, -1)
    upper = shift_ring(jnp.concatenate([below, own, above]), "z", 8, 3)
    lower = shift_ring(jnp.concatenate([own, above]), "z", 8, -3)
    return jnp.concatenate([own, above, upper, lower, below])


def along_z(blocks):
    return lax.all_to_all(blocks, "z", 0, 0, tiled=True)


def shards(tokens, cotangent, policy, anchor, moment, second, readout, pair_index, noisy_flags):
    core = lax.axis_index("core")
    low = lax.axis_index("xlo")
    high = lax.axis_index("xhi")
    rows, channels = policy.shape
    half, quarter = channels // 2, channels // 4
    features = tokens.shape[1]

    def piece(array):
        return lax.dynamic_slice_in_dim(array, (core * 2 + low) * quarter, quarter, axis=1)

    def joined_halves(plane):
        return plane.reshape(2, features, quarter)

    sent, own = gradient_blocks(core[None], cotangent, tokens)
    anchor_piece = lax.optimization_barrier(piece(anchor).astype(jnp.bfloat16))
    pair = jnp.stack([anchor_piece, shift_ring(anchor_piece, "y", 4, 1)])
    sent, pair = lax.optimization_barrier((sent, pair))
    arrived = lax.ppermute(sent, "core", SWAP)
    strip = jnp.concatenate([pair, shift_ring(pair, "y", 4, 2)])
    blocks = own.astype(jnp.float32) + arrived.astype(jnp.float32)
    blocks, strip = lax.optimization_barrier((blocks.astype(jnp.bfloat16), strip))
    plane = to_plane(blocks.reshape(16, quarter, 8 * rows))
    strips = gather_z(strip)
    plane, strips, tokens = lax.optimization_barrier((plane, strips, tokens))
    sibling = lax.ppermute(tokens, "core", SWAP)
    left, right = turn(strips, 1), turn(strips, -1)
    column = along_z(plane_sum(plane).reshape(8, rows, quarter))
    far_left, far_right = turn(left[:4], 1), turn(right[4:], -1)
    gradient_piece, message = policy_message(
        (core * 2 + low)[None], column, policy, moment, second
    )
    policy_column = along_z(message).reshape(8 * rows, quarter)
    policy_copies, far_left, far_right, sibling = lax.optimization_barrier(
        (plane_copies(policy_column), far_left, far_right, sibling)
    )
    policy_plane = to_plane(policy_copies)
    frozen = frozen_values(
        jnp.stack([high * 2 + low, lax.axis_index("y"), lax.axis_index("z")]), tokens, sibling, (strips, left, right, far_left, far_right)
    )

    readout_cols = lax.dynamic_slice_in_dim(readout, core * half, half)[None]
    parts = score_sums(tokens, sibling, joined_halves(policy_plane), frozen, readout_cols)
    parts, gradient_piece = lax.optimization_barrier((parts, gradient_piece))
    other = lax.ppermute(gradient_piece, "xlo", SWAP)
    strip = jnp.where(
        low == 0,
        jnp.concatenate([gradient_piece, other], axis=1),
        jnp.concatenate([other, gradient_piece], axis=1),
    )
    other = lax.ppermute(strip, "core", SWAP)
    gradient = jnp.where(
        core == 0,
        jnp.concatenate([strip, other], axis=1),
        jnp.concatenate([other, strip], axis=1),
    )
    policy_next, anchor_next, moment_next, second_next = adam_update(
        gradient, policy, anchor, moment, second
    )

    parts = lax.all_to_all(parts, AXES, 0, 0, tiled=True)
    parts = parts.reshape(2, 2, 64, 128)
    margins = (parts[:, :, :, :4] + parts[:, ::-1, :, 4:8]).reshape(-1)
    pair_loss = pair_losses(margins, pair_index, noisy_flags)
    return (policy_next, anchor_next, moment_next, second_next, pair_loss)


def solution(mesh):
    fine = Mesh(mesh.devices.reshape(2, 2, 4, 2, 8), AXES)
    everywhere = AXES
    owners = ("y", "xhi", "z")
    placed = (
        P(everywhere, None),
        P(everywhere, None),
        P(owners, None),
        P(owners, None),
        P(owners, None),
        P(owners, None),
        P(),
        P(everywhere, None),
        P(everywhere),
    )
    return jax.shard_map(
        shards,
        mesh=fine,
        in_specs=placed,
        out_specs=(
            P(owners, None),
            P(owners, None),
            P(owners, None),
            P(owners, None),
            P(everywhere),
        ),
        check_vma=False,
    )
```

```python
import functools

import jax
import jax.numpy as jnp
from jax import lax
from jax.experimental import pallas as pl
from jax.experimental.pallas import tpu as pltpu
from jax.sharding import Mesh
from jax.sharding import PartitionSpec as P

LEN = 192


beta_one = 0.9
beta_two = 0.95
step_count = 20
learn_rate = 0.003
adam_epsilon = 1e-08
blend_rate = 0.6
smoothing = 0.1

AXES = ("xlo", "core", "y", "xhi", "z")
PLANE = ("xlo", "y", "xhi")
SWAP = ((0, 1), (1, 0))


def policy_update(gradient, policy, moment, second):
    moment_new = beta_one * moment + (1.0 - beta_one) * gradient
    second_new = beta_two * second + (1.0 - beta_two) * gradient * gradient
    correct_one = 1.0 - beta_one**step_count
    correct_two = 1.0 - beta_two**step_count
    policy_new = policy - learn_rate * (moment_new / correct_one) / (
        jnp.sqrt(second_new / correct_two) + adam_epsilon
    )
    return (policy_new, moment_new, second_new)


def adam_update(gradient, policy, anchor, moment, second):
    policy_new, moment_new, second_new = policy_update(gradient, policy, moment, second)
    anchor_new = blend_rate * policy_new + (1.0 - blend_rate) * anchor
    return (policy_new, anchor_new, moment_new, second_new)


def pair_losses(margins, pair_index, noisy_flags):
    sequence_index = jnp.arange(margins.shape[0], dtype=jnp.int32)
    chosen = jnp.sum(
        jnp.where(pair_index[:, 0:1] == sequence_index[None, :], margins[None, :], 0.0), axis=1
    )
    rejected = jnp.sum(
        jnp.where(pair_index[:, 1:2] == sequence_index[None, :], margins[None, :], 0.0), axis=1
    )
    margin_gap = chosen - rejected
    logit_value = jnp.where(noisy_flags == 1, -margin_gap, margin_gap)
    return -(1.0 - smoothing) * jax.nn.log_sigmoid(logit_value) - smoothing * jax.nn.log_sigmoid(
        -logit_value
    )


VMEM = 32 << 20
VMEM_GRADIENT = 32 << 20
VMEM_SCORE = 32 << 20
AHEAD = 3


def in_hbm(array):
    return pltpu.with_memory_space_constraint(array, pltpu.HBM)


def gradient_kernel(part, place, cotangent, tokens, sent, own, held, turned, sems):
    channels = held.shape[1]
    half, quarter = channels // 2, channels // 4
    width = sent.shape[3]
    core = place[0]
    halves = [
        pltpu.make_async_copy(
            cotangent.at[:, pl.ds(pl.multiple_of(which * half, half), half)],
            held.at[:, pl.ds(at * half, half)],
            sems.at[at],
        )
        for at, which in enumerate((1 - core, core))
    ]
    blocks = [
        pltpu.make_async_copy(
            tokens.at[:, pl.ds((2 * at + part) * width, width)],
            turned.at[:, pl.ds(at * width, width)],
            sems.at[2 + at],
        )
        for at in range(8)
    ]
    for load in halves + blocks[:AHEAD]:
        load.start()
    for load in halves:
        load.wait()
    for at, load in enumerate(blocks):
        load.wait()
        if at + AHEAD < len(blocks):
            blocks[at + AHEAD].start()
        product = lax.dot_general(
            held[...],
            turned[:, at * width : (at + 1) * width],
            (((0,), (0,)), ((), ())),
            preferred_element_type=jnp.float32,
        ).astype(sent.dtype)
        sent[0, at] = product[:quarter]
        sent[1, at] = product[quarter:half]
        own[0, at] = product[half : half + quarter]
        own[1, at] = product[half + quarter :]


def gradient_blocks(part, place, cotangent, tokens):
    count, features = tokens.shape
    channels = cotangent.shape[1]
    quarter = channels // 4
    width = features // 16
    block = pltpu.VMEM((2, 8, quarter, width), jnp.bfloat16)
    return pl.pallas_call(
        functools.partial(gradient_kernel, part),
        in_specs=[
            pl.BlockSpec(memory_space=pltpu.SMEM),
            pl.BlockSpec(memory_space=pltpu.HBM),
            pl.BlockSpec(memory_space=pltpu.HBM),
        ],
        out_specs=[pl.BlockSpec(memory_space=pltpu.VMEM)] * 2,
        out_shape=[block, block],
        scratch_shapes=[
            pltpu.VMEM(cotangent.shape, cotangent.dtype),
            pltpu.VMEM((count, features // 2), tokens.dtype),
            pltpu.SemaphoreType.DMA((10,)),
        ],
        cost_estimate=pl.CostEstimate(
            flops=count * features * channels, bytes_accessed=6 << 20, transcendentals=0
        ),
        compiler_params=pltpu.CompilerParams(vmem_limit_bytes=VMEM_GRADIENT),
        name="gradient_blocks",
    )(place, in_hbm(cotangent), in_hbm(tokens))


def frozen_kernel(place, tokens, sibling, here, left, right, far_left, far_right, out, joined):
    depth, count, rows, quarter = here.shape

    @pl.when(pl.program_id(0) == 0)
    def _():
        for shift, ref, first in (
            (0, here, 0), (3, left, 0), (1, right, 0), (2, far_left, 0), (2, far_right, depth // 2)
        ):
            chip = (place[0] + shift) % 4
            lanes = pl.ds(pl.multiple_of((chip % 2) * quarter, quarter), quarter)
            for at in range(ref.shape[0]):
                level = (place[2] + first + at) % 8
                for turn_y in range(count):
                    owner = ((place[1] + turn_y) % 4) * 16 + (chip // 2) * 8 + level
                    span = pl.ds(pl.multiple_of(owner * rows, rows), rows)
                    joined[span, lanes] = ref[at, turn_y]

    for ref, turn_of in ((tokens, pl.program_id(0) < 2), (sibling, pl.program_id(0) >= 2)):

        @pl.when(turn_of)
        def _():
            out[...] = jnp.dot(ref[...], joined[...], preferred_element_type=jnp.float32)


def sigmoid_sums(values):
    rows = values.reshape(LEN // 8, 8, values.shape[1])
    lows = jnp.minimum(rows, 0.0)
    factors = 1.0 + jnp.exp(-jnp.abs(rows))
    low_sum, product = lows[0], factors[0]
    for step in range(1, LEN // 8):
        low_sum = low_sum + lows[step]
        product = product * factors[step]
    return low_sum - jnp.log(product)


def score_kernel(tokens, sibling, halves, frozen, readout, out, joined, held, still, sems):
    quarter = halves.shape[-1]
    count = tokens.shape[0]
    sizes = (2 * LEN,) * 4
    loads, at = [], 0
    for step, size in enumerate(sizes):
        source, first = (tokens, at) if at < count else (sibling, at - count)
        span = pl.ds(at, size)
        loads.append(
            (
                pltpu.make_async_copy(
                    source.at[pl.ds(first, size)], held.at[span], sems.at[2 * step]
                ),
                pltpu.make_async_copy(frozen.at[span], still.at[span], sems.at[2 * step + 1]),
            )
        )
        at += size
    for pair in loads[:2]:
        for load in pair:
            load.start()
    joined[:, :quarter] = halves[0]
    joined[:, quarter:] = halves[1]
    scale = readout[...]
    lane = lax.broadcasted_iota(jnp.int32, (1, 128), 1)
    parts = jnp.zeros((1, 128), jnp.float32)
    at = 0
    for step, size in enumerate(sizes):
        for load in loads[step]:
            load.wait()
        for load in loads[step + 2] if step + 2 < len(sizes) else ():
            load.start()
        values = jnp.dot(held[at : at + size], joined[...], preferred_element_type=jnp.float32)
        blended = blend_rate * values + (1.0 - blend_rate) * still[at : at + size]
        values, blended = values * scale, blended * scale
        for first in range(0, size, LEN):
            rows = slice(first, first + LEN)
            gap = sigmoid_sums(values[rows]) - sigmoid_sums(blended[rows])
            parts = jnp.where(lane == (at + first) // LEN, jnp.sum(gap) / LEN, parts)
        at += size
    out[...] = jnp.broadcast_to(parts[None], out.shape)


def token_specs(count, features):
    rows = count // 2
    return [
        pl.BlockSpec((rows, features), lambda i, *_: (jnp.minimum(i, 1), 0)),
        pl.BlockSpec((rows, features), lambda i, *_: (jnp.maximum(i - 2, 0), 0)),
    ]


def frozen_values(place, tokens, sibling, strips):
    count, features = tokens.shape
    width = 2 * strips[0].shape[-1]
    return pl.pallas_call(
        frozen_kernel,
        grid_spec=pltpu.PrefetchScalarGridSpec(
            num_scalar_prefetch=1,
            grid=(4,),
            in_specs=token_specs(count, features)
            + [pl.BlockSpec(strip.shape, lambda i, *_: (0, 0, 0, 0)) for strip in strips],
            out_specs=pl.BlockSpec((count // 2, width), lambda i, *_: (i, 0)),
            scratch_shapes=[pltpu.VMEM((features, width), jnp.bfloat16)],
        ),
        out_shape=jax.ShapeDtypeStruct((2 * count, width), jnp.float32),
        cost_estimate=pl.CostEstimate(
            flops=4 * count * features * width, bytes_accessed=16 << 20, transcendentals=0
        ),
        compiler_params=pltpu.CompilerParams(vmem_limit_bytes=VMEM),
        name="frozen_values",
    )(place, in_hbm(tokens), in_hbm(sibling), *strips)


def score_sums(tokens, sibling, halves, frozen, readout):
    count, features = tokens.shape
    width = 2 * halves.shape[-1]
    return pl.pallas_call(
        score_kernel,
        out_shape=jax.ShapeDtypeStruct((256, 1, 128), jnp.float32),
        in_specs=[
            pl.BlockSpec(memory_space=pltpu.HBM),
            pl.BlockSpec(memory_space=pltpu.HBM),
            pl.BlockSpec(memory_space=pltpu.VMEM),
            pl.BlockSpec(memory_space=pltpu.HBM),
            pl.BlockSpec(memory_space=pltpu.VMEM),
        ],
        scratch_shapes=[
            pltpu.VMEM((features, width), jnp.bfloat16),
            pltpu.VMEM((2 * count, features), tokens.dtype),
            pltpu.VMEM(frozen.shape, frozen.dtype),
            pltpu.SemaphoreType.DMA((8,)),
        ],
        cost_estimate=pl.CostEstimate(
            flops=4 * count * features * width, bytes_accessed=16 << 20, transcendentals=0
        ),
        compiler_params=pltpu.CompilerParams(vmem_limit_bytes=VMEM_SCORE),
        name="score_sums",
    )(in_hbm(tokens), in_hbm(sibling), halves, in_hbm(frozen), readout)


def plane_sum_kernel(blocks, out):
    total = blocks[0].astype(jnp.float32)
    for at in range(1, blocks.shape[0]):
        total = total + blocks[at].astype(jnp.float32)
    out[...] = total.T.astype(out.dtype)


def plane_sum(blocks):
    _, channels, features = blocks.shape
    return pl.pallas_call(
        plane_sum_kernel,
        out_shape=jax.ShapeDtypeStruct((features, channels), jnp.bfloat16),
        compiler_params=pltpu.CompilerParams(vmem_limit_bytes=16 << 20),
        name="plane_sum",
    )(blocks)


def policy_kernel(place, column, policy, moment, second, gradient_out, message):
    quarter = column.shape[2]
    lanes = pl.ds(pl.multiple_of(place[0] * quarter, quarter), quarter)
    gradient = column[0].astype(jnp.float32)
    for at in range(1, column.shape[0]):
        gradient = gradient + column[at].astype(jnp.float32)
    gradient_out[...] = gradient
    updated = policy_update(gradient, policy[:, lanes], moment[:, lanes], second[:, lanes])[0]
    for at in range(message.shape[0]):
        message[at] = updated.astype(message.dtype)


def policy_message(place, column, policy, moment, second):
    return pl.pallas_call(
        policy_kernel,
        in_specs=[pl.BlockSpec(memory_space=pltpu.SMEM)]
        + [pl.BlockSpec(memory_space=pltpu.VMEM)] * 4,
        out_shape=[
            jax.ShapeDtypeStruct(column.shape[1:], jnp.float32),
            jax.ShapeDtypeStruct(column.shape, column.dtype),
        ],
        compiler_params=pltpu.CompilerParams(vmem_limit_bytes=16 << 20),
        name="policy_message",
    )(place, column, policy, moment, second)


def copies_kernel(column, out, sems):
    sends = [pltpu.make_async_copy(column, out.at[at], sems.at[at]) for at in range(out.shape[0])]
    for send in sends:
        send.start()
    for send in sends:
        send.wait()


def plane_copies(column):
    return pl.pallas_call(
        copies_kernel,
        in_specs=[pl.BlockSpec(memory_space=pltpu.VMEM)],
        out_specs=pl.BlockSpec(memory_space=pltpu.HBM),
        out_shape=jax.ShapeDtypeStruct((16,) + column.shape, column.dtype),
        scratch_shapes=[pltpu.SemaphoreType.DMA((16,))],
        compiler_params=pltpu.CompilerParams(vmem_limit_bytes=16 << 20),
        name="plane_copies",
    )(column)


def to_plane(blocks):
    return lax.all_to_all(blocks, PLANE, 0, 0, tiled=True)


def turn(block, shift):
    def index(x):
        return (x % 2) * 2 + x // 2

    return lax.ppermute(
        block, ("xlo", "xhi"), [(index(x), index((x + shift) % 4)) for x in range(4)]
    )


def shift_ring(block, axis, size, shift):
    return lax.ppermute(block, axis, [(i, (i - shift) % size) for i in range(size)])


def gather_z(own):
    own = own[None]
    above, below = shift_ring(own, "z", 8, 1), shift_ring(own, "z", 8, -1)
    upper = shift_ring(jnp.concatenate([below, own, above]), "z", 8, 3)
    lower = shift_ring(jnp.concatenate([own, above]), "z", 8, -3)
    return jnp.concatenate([own, above, upper, lower, below])


def along_z(blocks):
    return lax.all_to_all(blocks, "z", 0, 0, tiled=True)


def shards(tokens, cotangent, policy, anchor, moment, second, readout, pair_index, noisy_flags):
    core = lax.axis_index("core")
    low = lax.axis_index("xlo")
    high = lax.axis_index("xhi")
    rows, channels = policy.shape
    half, quarter = channels // 2, channels // 4
    features = tokens.shape[1]

    def piece(array):
        return lax.dynamic_slice_in_dim(array, (core * 2 + low) * quarter, quarter, axis=1)

    def joined_halves(plane):
        return plane.reshape(2, features, quarter)

    sent, own = gradient_blocks(0, core[None], cotangent, tokens)
    anchor_piece = lax.optimization_barrier(piece(anchor).astype(jnp.bfloat16))
    pair = jnp.stack([anchor_piece, shift_ring(anchor_piece, "y", 4, 1)])
    sent, pair = lax.optimization_barrier((sent, pair))
    arrived = lax.ppermute(sent, "core", SWAP)
    strip = jnp.concatenate([pair, shift_ring(pair, "y", 4, 2)])
    sent, own_upper = gradient_blocks(1, core[None], cotangent, tokens)
    sent, arrived, strip = lax.optimization_barrier((sent, arrived, strip))
    arrived_upper = lax.ppermute(sent, "core", SWAP)
    blocks = jnp.concatenate(
        [
            (mine.astype(jnp.float32) + other.astype(jnp.float32)).astype(jnp.bfloat16)
            for mine, other in ((own, arrived), (own_upper, arrived_upper))
        ],
        axis=3,
    )
    blocks, strip = lax.optimization_barrier((blocks, strip))
    plane = to_plane(blocks.reshape(16, quarter, 8 * rows))
    strips = gather_z(strip)
    plane, strips, tokens = lax.optimization_barrier((plane, strips, tokens))
    sibling = lax.ppermute(tokens, "core", SWAP)
    left, right = turn(strips, 1), turn(strips, -1)
    column = along_z(plane_sum(plane).reshape(8, rows, quarter))
    far_left, far_right = turn(left[:4], 1), turn(right[4:], -1)
    gradient_piece, message = policy_message(
        (core * 2 + low)[None], column, policy, moment, second
    )
    policy_column = along_z(message).reshape(8 * rows, quarter)
    policy_copies, far_left, far_right, sibling = lax.optimization_barrier(
        (plane_copies(policy_column), far_left, far_right, sibling)
    )
    policy_plane = to_plane(policy_copies)
    frozen = frozen_values(
        jnp.stack([high * 2 + low, lax.axis_index("y"), lax.axis_index("z")]), tokens, sibling, (strips, left, right, far_left, far_right)
    )

    readout_cols = lax.dynamic_slice_in_dim(readout, core * half, half)[None]
    parts = score_sums(tokens, sibling, joined_halves(policy_plane), frozen, readout_cols)
    parts, gradient_piece = lax.optimization_barrier((parts, gradient_piece))
    other = lax.ppermute(gradient_piece, "xlo", SWAP)
    strip = jnp.where(
        low == 0,
        jnp.concatenate([gradient_piece, other], axis=1),
        jnp.concatenate([other, gradient_piece], axis=1),
    )
    other = lax.ppermute(strip, "core", SWAP)
    gradient = jnp.where(
        core == 0,
        jnp.concatenate([strip, other], axis=1),
        jnp.concatenate([other, strip], axis=1),
    )
    policy_next, anchor_next, moment_next, second_next = adam_update(
        gradient, policy, anchor, moment, second
    )

    parts = lax.all_to_all(parts, AXES, 0, 0, tiled=True)
    parts = parts.reshape(2, 2, 64, 128)
    margins = (parts[:, :, :, :4] + parts[:, ::-1, :, 4:8]).reshape(-1)
    pair_loss = pair_losses(margins, pair_index, noisy_flags)
    return (policy_next, anchor_next, moment_next, second_next, pair_loss)


def solution(mesh):
    fine = Mesh(mesh.devices.reshape(2, 2, 4, 2, 8), AXES)
    everywhere = AXES
    owners = ("y", "xhi", "z")
    placed = (
        P(everywhere, None),
        P(everywhere, None),
        P(owners, None),
        P(owners, None),
        P(owners, None),
        P(owners, None),
        P(),
        P(everywhere, None),
        P(everywhere),
    )
    return jax.shard_map(
        shards,
        mesh=fine,
        in_specs=placed,
        out_specs=(
            P(owners, None),
            P(owners, None),
            P(owners, None),
            P(owners, None),
            P(everywhere),
        ),
        check_vma=False,
    )
```

```python
import jax
import jax.numpy as jnp
from jax import lax
from jax.experimental import pallas as pl
from jax.experimental.pallas import tpu as pltpu
from jax.sharding import Mesh
from jax.sharding import PartitionSpec as P

LEN = 192


beta_one = 0.9
beta_two = 0.95
step_count = 20
learn_rate = 0.003
adam_epsilon = 1e-08
blend_rate = 0.6
smoothing = 0.1

AXES = ("xlo", "core", "y", "xhi", "z")
PLANE = ("xlo", "y", "xhi")
SWAP = ((0, 1), (1, 0))


def policy_update(gradient, policy, moment, second):
    moment_new = beta_one * moment + (1.0 - beta_one) * gradient
    second_new = beta_two * second + (1.0 - beta_two) * gradient * gradient
    correct_one = 1.0 - beta_one**step_count
    correct_two = 1.0 - beta_two**step_count
    policy_new = policy - learn_rate * (moment_new / correct_one) / (
        jnp.sqrt(second_new / correct_two) + adam_epsilon
    )
    return (policy_new, moment_new, second_new)


def adam_update(gradient, policy, anchor, moment, second):
    policy_new, moment_new, second_new = policy_update(gradient, policy, moment, second)
    anchor_new = blend_rate * policy_new + (1.0 - blend_rate) * anchor
    return (policy_new, anchor_new, moment_new, second_new)


def pair_losses(margins, pair_index, noisy_flags):
    sequence_index = jnp.arange(margins.shape[0], dtype=jnp.int32)
    chosen = jnp.sum(
        jnp.where(pair_index[:, 0:1] == sequence_index[None, :], margins[None, :], 0.0), axis=1
    )
    rejected = jnp.sum(
        jnp.where(pair_index[:, 1:2] == sequence_index[None, :], margins[None, :], 0.0), axis=1
    )
    margin_gap = chosen - rejected
    logit_value = jnp.where(noisy_flags == 1, -margin_gap, margin_gap)
    return -(1.0 - smoothing) * jax.nn.log_sigmoid(logit_value) - smoothing * jax.nn.log_sigmoid(
        -logit_value
    )


VMEM = 32 << 20
VMEM_GRADIENT = 32 << 20
VMEM_SCORE = 32 << 20
AHEAD = 3


def in_hbm(array):
    return pltpu.with_memory_space_constraint(array, pltpu.HBM)


def gradient_kernel(place, cotangent, tokens, sent, own, held, turned, sems):
    channels = held.shape[1]
    half, quarter = channels // 2, channels // 4
    width = sent.shape[3]
    core = place[0]
    halves = [
        pltpu.make_async_copy(
            cotangent.at[:, pl.ds(pl.multiple_of(which * half, half), half)],
            held.at[:, pl.ds(at * half, half)],
            sems.at[at],
        )
        for at, which in enumerate((1 - core, core))
    ]
    blocks = [
        pltpu.make_async_copy(
            tokens.at[:, pl.ds(at * width, width)],
            turned.at[:, pl.ds(at * width, width)],
            sems.at[2 + at],
        )
        for at in range(8)
    ]
    for load in halves + blocks[:AHEAD]:
        load.start()
    for load in halves:
        load.wait()
    for at, load in enumerate(blocks):
        load.wait()
        if at + AHEAD < len(blocks):
            blocks[at + AHEAD].start()
        product = lax.dot_general(
            held[...],
            turned[:, at * width : (at + 1) * width],
            (((0,), (0,)), ((), ())),
            preferred_element_type=jnp.float32,
        ).astype(sent.dtype)
        sent[0, at] = product[:quarter]
        sent[1, at] = product[quarter:half]
        own[0, at] = product[half : half + quarter]
        own[1, at] = product[half + quarter :]


def gradient_blocks(place, cotangent, tokens):
    count, features = tokens.shape
    channels = cotangent.shape[1]
    quarter = channels // 4
    width = features // 8
    block = pltpu.VMEM((2, 8, quarter, width), jnp.bfloat16)
    return pl.pallas_call(
        gradient_kernel,
        in_specs=[
            pl.BlockSpec(memory_space=pltpu.SMEM),
            pl.BlockSpec(memory_space=pltpu.HBM),
            pl.BlockSpec(memory_space=pltpu.HBM),
        ],
        out_specs=[pl.BlockSpec(memory_space=pltpu.VMEM)] * 2,
        out_shape=[block, block],
        scratch_shapes=[
            pltpu.VMEM(cotangent.shape, cotangent.dtype),
            pltpu.VMEM(tokens.shape, tokens.dtype),
            pltpu.SemaphoreType.DMA((10,)),
        ],
        cost_estimate=pl.CostEstimate(
            flops=2 * count * features * channels, bytes_accessed=12 << 20, transcendentals=0
        ),
        compiler_params=pltpu.CompilerParams(vmem_limit_bytes=VMEM_GRADIENT),
        name="gradient_blocks",
    )(place, in_hbm(cotangent), in_hbm(tokens))


def frozen_kernel(place, tokens, sibling, here, left, right, far_left, far_right, out, joined):
    depth, count, rows, quarter = here.shape

    @pl.when(pl.program_id(0) == 0)
    def _():
        for shift, ref, first in (
            (0, here, 0), (3, left, 0), (1, right, 0), (2, far_left, 0), (2, far_right, depth // 2)
        ):
            chip = (place[0] + shift) % 4
            lanes = pl.ds(pl.multiple_of((chip % 2) * quarter, quarter), quarter)
            for at in range(ref.shape[0]):
                level = (place[2] + first + at) % 8
                for turn_y in range(count):
                    owner = ((place[1] + turn_y) % 4) * 16 + (chip // 2) * 8 + level
                    span = pl.ds(pl.multiple_of(owner * rows, rows), rows)
                    joined[span, lanes] = ref[at, turn_y]

    for ref, turn_of in ((tokens, pl.program_id(0) < 2), (sibling, pl.program_id(0) >= 2)):

        @pl.when(turn_of)
        def _():
            out[...] = jnp.dot(ref[...], joined[...], preferred_element_type=jnp.float32)


def sigmoid_sums(values):
    rows = values.reshape(LEN // 8, 8, values.shape[1])
    lows = jnp.minimum(rows, 0.0)
    factors = 1.0 + jnp.exp(-jnp.abs(rows))
    low_sum, product = lows[0], factors[0]
    for step in range(1, LEN // 8):
        low_sum = low_sum + lows[step]
        product = product * factors[step]
    return low_sum - jnp.log(product)


def score_kernel(tokens, sibling, halves, frozen, readout, out, joined, held, still, sems):
    quarter = halves.shape[-1]
    count = tokens.shape[0]
    sizes = (2 * LEN,) * 4
    loads, at = [], 0
    for step, size in enumerate(sizes):
        source, first = (tokens, at) if at < count else (sibling, at - count)
        span = pl.ds(at, size)
        loads.append(
            (
                pltpu.make_async_copy(
                    source.at[pl.ds(first, size)], held.at[span], sems.at[2 * step]
                ),
                pltpu.make_async_copy(frozen.at[span], still.at[span], sems.at[2 * step + 1]),
            )
        )
        at += size
    for pair in loads[:2]:
        for load in pair:
            load.start()
    joined[:, :quarter] = halves[0]
    joined[:, quarter:] = halves[1]
    scale = readout[...]
    lane = lax.broadcasted_iota(jnp.int32, (1, 128), 1)
    parts = jnp.zeros((1, 128), jnp.float32)
    at = 0
    for step, size in enumerate(sizes):
        for load in loads[step]:
            load.wait()
        for load in loads[step + 2] if step + 2 < len(sizes) else ():
            load.start()
        values = jnp.dot(held[at : at + size], joined[...], preferred_element_type=jnp.float32)
        blended = blend_rate * values + (1.0 - blend_rate) * still[at : at + size]
        values, blended = values * scale, blended * scale
        for first in range(0, size, LEN):
            rows = slice(first, first + LEN)
            gap = sigmoid_sums(values[rows]) - sigmoid_sums(blended[rows])
            parts = jnp.where(lane == (at + first) // LEN, jnp.sum(gap) / LEN, parts)
        at += size
    out[...] = jnp.broadcast_to(parts[None], out.shape)


def token_specs(count, features):
    rows = count // 2
    return [
        pl.BlockSpec((rows, features), lambda i, *_: (jnp.minimum(i, 1), 0)),
        pl.BlockSpec((rows, features), lambda i, *_: (jnp.maximum(i - 2, 0), 0)),
    ]


def frozen_values(place, tokens, sibling, strips):
    count, features = tokens.shape
    width = 2 * strips[0].shape[-1]
    return pl.pallas_call(
        frozen_kernel,
        grid_spec=pltpu.PrefetchScalarGridSpec(
            num_scalar_prefetch=1,
            grid=(4,),
            in_specs=token_specs(count, features)
            + [pl.BlockSpec(strip.shape, lambda i, *_: (0, 0, 0, 0)) for strip in strips],
            out_specs=pl.BlockSpec((count // 2, width), lambda i, *_: (i, 0)),
            scratch_shapes=[pltpu.VMEM((features, width), jnp.bfloat16)],
        ),
        out_shape=jax.ShapeDtypeStruct((2 * count, width), jnp.float32),
        cost_estimate=pl.CostEstimate(
            flops=4 * count * features * width, bytes_accessed=16 << 20, transcendentals=0
        ),
        compiler_params=pltpu.CompilerParams(vmem_limit_bytes=VMEM),
        name="frozen_values",
    )(place, in_hbm(tokens), in_hbm(sibling), *strips)


def score_sums(tokens, sibling, halves, frozen, readout):
    count, features = tokens.shape
    width = 2 * halves.shape[-1]
    return pl.pallas_call(
        score_kernel,
        out_shape=jax.ShapeDtypeStruct((256, 1, 128), jnp.float32),
        in_specs=[
            pl.BlockSpec(memory_space=pltpu.HBM),
            pl.BlockSpec(memory_space=pltpu.HBM),
            pl.BlockSpec(memory_space=pltpu.VMEM),
            pl.BlockSpec(memory_space=pltpu.HBM),
            pl.BlockSpec(memory_space=pltpu.VMEM),
        ],
        scratch_shapes=[
            pltpu.VMEM((features, width), jnp.bfloat16),
            pltpu.VMEM((2 * count, features), tokens.dtype),
            pltpu.VMEM(frozen.shape, frozen.dtype),
            pltpu.SemaphoreType.DMA((8,)),
        ],
        cost_estimate=pl.CostEstimate(
            flops=4 * count * features * width, bytes_accessed=16 << 20, transcendentals=0
        ),
        compiler_params=pltpu.CompilerParams(vmem_limit_bytes=VMEM_SCORE),
        name="score_sums",
    )(in_hbm(tokens), in_hbm(sibling), halves, in_hbm(frozen), readout)


def plane_sum_kernel(blocks, out):
    total = blocks[0].astype(jnp.float32)
    for at in range(1, blocks.shape[0]):
        total = total + blocks[at].astype(jnp.float32)
    out[...] = total.T.astype(out.dtype)


def plane_sum(blocks):
    _, channels, features = blocks.shape
    return pl.pallas_call(
        plane_sum_kernel,
        out_shape=jax.ShapeDtypeStruct((features, channels), jnp.bfloat16),
        compiler_params=pltpu.CompilerParams(vmem_limit_bytes=16 << 20),
        name="plane_sum",
    )(blocks)


def policy_kernel(place, column, policy, moment, second, gradient_out, message):
    quarter = column.shape[2]
    lanes = pl.ds(pl.multiple_of(place[0] * quarter, quarter), quarter)
    gradient = column[0].astype(jnp.float32)
    for at in range(1, column.shape[0]):
        gradient = gradient + column[at].astype(jnp.float32)
    gradient_out[...] = gradient
    updated = policy_update(gradient, policy[:, lanes], moment[:, lanes], second[:, lanes])[0]
    for at in range(message.shape[0]):
        message[at] = updated.astype(message.dtype)


def policy_message(place, column, policy, moment, second):
    return pl.pallas_call(
        policy_kernel,
        in_specs=[pl.BlockSpec(memory_space=pltpu.SMEM)]
        + [pl.BlockSpec(memory_space=pltpu.VMEM)] * 4,
        out_shape=[
            jax.ShapeDtypeStruct(column.shape[1:], jnp.float32),
            jax.ShapeDtypeStruct(column.shape, column.dtype),
        ],
        compiler_params=pltpu.CompilerParams(vmem_limit_bytes=16 << 20),
        name="policy_message",
    )(place, column, policy, moment, second)


def to_plane(blocks):
    return lax.all_to_all(blocks, PLANE, 0, 0, tiled=True)


def turn(block, shift):
    def index(x):
        return (x % 2) * 2 + x // 2

    return lax.ppermute(
        block, ("xlo", "xhi"), [(index(x), index((x + shift) % 4)) for x in range(4)]
    )


def shift_ring(block, axis, size, shift):
    return lax.ppermute(block, axis, [(i, (i - shift) % size) for i in range(size)])


def gather_z(own):
    own = own[None]
    above, below = shift_ring(own, "z", 8, 1), shift_ring(own, "z", 8, -1)
    upper = shift_ring(jnp.concatenate([below, own, above]), "z", 8, 3)
    lower = shift_ring(jnp.concatenate([own, above]), "z", 8, -3)
    return jnp.concatenate([own, above, upper, lower, below])


def along_z(blocks):
    return lax.all_to_all(blocks, "z", 0, 0, tiled=True)


def shards(tokens, cotangent, policy, anchor, moment, second, readout, pair_index, noisy_flags):
    core = lax.axis_index("core")
    low = lax.axis_index("xlo")
    high = lax.axis_index("xhi")
    rows, channels = policy.shape
    half, quarter = channels // 2, channels // 4
    features = tokens.shape[1]

    def piece(array):
        return lax.dynamic_slice_in_dim(array, (core * 2 + low) * quarter, quarter, axis=1)

    def copies(column):
        return jnp.broadcast_to(column[None], (16,) + column.shape)

    def joined_halves(plane):
        return plane.reshape(2, features, quarter)

    sent, own = gradient_blocks(core[None], cotangent, tokens)
    anchor_piece = lax.optimization_barrier(piece(anchor).astype(jnp.bfloat16))
    pair = jnp.stack([anchor_piece, shift_ring(anchor_piece, "y", 4, 1)])
    sent, pair = lax.optimization_barrier((sent, pair))
    arrived = lax.ppermute(sent, "core", SWAP)
    strip = jnp.concatenate([pair, shift_ring(pair, "y", 4, 2)])
    blocks = own.astype(jnp.float32) + arrived.astype(jnp.float32)
    blocks, strip = lax.optimization_barrier((blocks.astype(jnp.bfloat16), strip))
    plane = to_plane(blocks.reshape(16, quarter, 8 * rows))
    strips = gather_z(strip)
    plane, strips, tokens = lax.optimization_barrier((plane, strips, tokens))
    sibling = lax.ppermute(tokens, "core", SWAP)
    left, right = turn(strips, 1), turn(strips, -1)
    column = along_z(plane_sum(plane).reshape(8, rows, quarter))
    far_left, far_right = turn(left[:4], 1), turn(right[4:], -1)
    gradient_piece, message = policy_message(
        (core * 2 + low)[None], column, policy, moment, second
    )
    policy_column = along_z(message).reshape(8 * rows, quarter)
    other = lax.ppermute(gradient_piece, "xlo", SWAP)
    policy_copies, far_left, far_right, sibling, other = lax.optimization_barrier(
        (copies(policy_column), far_left, far_right, sibling, other)
    )
    policy_plane = to_plane(policy_copies)
    frozen = frozen_values(
        jnp.stack([high * 2 + low, lax.axis_index("y"), lax.axis_index("z")]), tokens, sibling, (strips, left, right, far_left, far_right)
    )

    strip = jnp.where(
        low == 0,
        jnp.concatenate([gradient_piece, other], axis=1),
        jnp.concatenate([other, gradient_piece], axis=1),
    )
    other = lax.ppermute(strip, "core", SWAP)
    gradient = jnp.where(
        core == 0,
        jnp.concatenate([strip, other], axis=1),
        jnp.concatenate([other, strip], axis=1),
    )
    policy_next, anchor_next, moment_next, second_next = adam_update(
        gradient, policy, anchor, moment, second
    )

    readout_cols = lax.dynamic_slice_in_dim(readout, core * half, half)[None]
    parts = score_sums(tokens, sibling, joined_halves(policy_plane), frozen, readout_cols)
    parts = lax.all_to_all(parts, AXES, 0, 0, tiled=True)
    parts = parts.reshape(2, 2, 64, 128)
    margins = (parts[:, :, :, :4] + parts[:, ::-1, :, 4:8]).reshape(-1)
    pair_loss = pair_losses(margins, pair_index, noisy_flags)
    return (policy_next, anchor_next, moment_next, second_next, pair_loss)


def solution(mesh):
    fine = Mesh(mesh.devices.reshape(2, 2, 4, 2, 8), AXES)
    everywhere = AXES
    owners = ("y", "xhi", "z")
    placed = (
        P(everywhere, None),
        P(everywhere, None),
        P(owners, None),
        P(owners, None),
        P(owners, None),
        P(owners, None),
        P(),
        P(everywhere, None),
        P(everywhere),
    )
    return jax.shard_map(
        shards,
        mesh=fine,
        in_specs=placed,
        out_specs=(
            P(owners, None),
            P(owners, None),
            P(owners, None),
            P(owners, None),
            P(everywhere),
        ),
        check_vma=False,
    )
```
